32 devices in a mesh: groups: 2 (over y), seq: 4 (over z), dp: 2 (over x), tensor: 2 (over core).
Axes of the slice: x: 2, y: 2, z: 4, core: 2. Of those that a mesh axis runs over, the one named last changes fastest.
Arguments:
- tokens: bfloat16 [4, 512, 2048], P(('groups', 'dp'), 'seq', 'tensor'), parts along dimension 0, may hold values from -6 to 6
- grad_out: bfloat16 [4, 512, 2048], P(('groups', 'dp'), 'seq', 'tensor'), parts along dimension 0, may hold values from -6 to 6
- picks: int32 [4, 64], P(('groups', 'dp')), parts along dimension 0, may hold values from 0 to 511, as said below
- scores: float32 [4, 64], P(('groups', 'dp')), parts along dimension 0, may hold values from 0.1 to 1
- w_gate: bfloat16 [2048, 1792], P('dp', ('seq', 'tensor')), may hold values from -0.125 to 0.125
- w_up: bfloat16 [2048, 1792], P('dp', ('seq', 'tensor')), may hold values from -0.125 to 0.125
- w_down: bfloat16 [1792, 2048], P(('seq', 'tensor'), 'dp'), may hold values from -0.125 to 0.125
Outputs:
- grad_tokens: bfloat16 [4, 512, 2048], P(('groups', 'dp'), 'seq', 'tensor'), parts along dimension 0
- grad_gate: bfloat16 [4096, 1792], P(('groups', 'dp'), ('seq', 'tensor')), parts along dimension 0
- grad_up: bfloat16 [4096, 1792], P(('groups', 'dp'), ('seq', 'tensor')), parts along dimension 0
- grad_down: bfloat16 [3584, 2048], P(('groups', 'seq', 'tensor'), 'dp'), parts along dimension 0
The draws below stay inside these ranges and needn't reach their ends.
There are 2 independent parts, one for each index of `groups`. The reference program is written for one: setup_inputs(seed, part) draws one part's arguments, and reference() takes and returns one part's arrays. A program takes and returns all parts, laid end to end along the dimension named above; an argument that names none is the same for every part. Nothing has to cross between parts.
Inputs may be any that keep to these rules, and one draw needn't show every extreme that they name: Each row lists 64 different positions, in an order drawn from the seed. Among the positions k * 128 to (k + 1) * 128 - 1 of one shard lie at most 32 picks of a row, and in every row one shard holds exactly 32.
All inputs are finite; a program needn't handle non-finite values.
Results may differ from the reference program's by a relative error of at most 0.0066.
Values may be sent and summed in bfloat16 or wider, within the bound.
No kernel may reach another device: no remote copies, remote signals or barrier semaphores. Data moves between devices by JAX's collectives and lax.ppermute only.
A program may use at most 64 MiB of HBM per device.

```python
import math
import jax
import jax.numpy as jnp
from jax import lax

D = 2048
TOK_DEV = 128
FF = 1792
TOKENS = 512
PICK_DEV = 16
CAP = 64
MOST = 32
N_SEQ = 4
N_DP = 2


def draw_picks(key, part):
    key = jax.random.fold_in(key, 7)

    def one_row(sub):
        key_order, key_delta, key_perm, key_shuffle = jax.random.split(sub, 4)
        order = jax.random.permutation(key_order, N_SEQ).astype(jnp.int32)
        delta = jax.random.randint(key_delta, (N_SEQ,), 0, PICK_DEV, dtype=jnp.int32)
        first = jax.random.randint(key_delta, (), 0, PICK_DEV + 1, dtype=jnp.int32)
        ranks = jnp.arange(N_SEQ, dtype=jnp.int32)
        pair_delta = jnp.take(delta, jnp.maximum(ranks - 4, 0) // 2)
        signs = jnp.where((ranks - 4) % 2 == 0, 1, -1).astype(jnp.int32)
        counts_rank = jnp.where(ranks >= 4, PICK_DEV + signs * pair_delta, PICK_DEV)
        counts_rank = jnp.where(ranks == 0, MOST, counts_rank)
        counts_rank = jnp.where(ranks == 1, first, counts_rank)
        counts_rank = jnp.where(ranks == 2, PICK_DEV - first, counts_rank)
        counts = jnp.take(counts_rank, jnp.argsort(order))
        perm_keys = jax.random.split(key_perm, N_SEQ)
        perms = jax.vmap(lambda k: jax.random.permutation(k, TOK_DEV))(perm_keys).astype(jnp.int32)
        where_at = jnp.argsort(perms, axis=1).astype(jnp.int32)
        chosen = where_at < counts[:, None]
        listed = jnp.nonzero(chosen.reshape(-1), size=CAP)[0].astype(jnp.int32)
        shuffle = jax.random.permutation(key_shuffle, CAP).astype(jnp.int32)
        return jnp.take(listed, shuffle)
    return jax.vmap(one_row)(jax.random.split(key, N_DP)).astype(jnp.int32)


def levels(own_key, extent, cuts, smallest, top_value):
    loudness = 1.0
    for axis_at, parts in cuts:
        steps = jax.random.uniform(jax.random.fold_in(jax.random.fold_in(own_key, 6), axis_at), (parts,), jnp.float32, smallest / len(cuts), top_value / len(cuts))
        loudness = loudness * jnp.repeat(jnp.exp(steps), extent[axis_at] // parts).reshape((-1,) + (1,) * (len(extent) - 1 - axis_at))
    return loudness


def normal_values(stream_key, shape, width, reach, cuts=(), held_as=jnp.bfloat16):
    drawn = width * jax.random.normal(stream_key, shape, jnp.float32)
    if cuts:
        drawn = drawn * levels(stream_key, shape, cuts, -0.22, 0.18)
    return jnp.clip(drawn, -reach, reach).astype(held_as)


def setup_inputs(seed: int = 0, part: int = 0) -> dict:
    streams_of = jax.random.split(jax.random.key(seed), 8)
    part_splits = jax.random.split(jax.random.fold_in(streams_of[7], part), 8)
    tokens = normal_values(part_splits[0], (N_DP, TOKENS, D), 1.0, 6.0, ((0, 2), (1, 4), (2, 2)))
    grad_out = normal_values(part_splits[1], (N_DP, TOKENS, D), 1.0, 6.0, ((0, 2), (1, 4), (2, 2)))
    picks = draw_picks(jax.random.fold_in(jax.random.fold_in(streams_of[7], part), 71), part)
    scores = jnp.clip(jnp.exp(math.log(1.0) - 2.3025851 * jax.random.uniform(part_splits[3], (N_DP, CAP), jnp.float32) ** levels(part_splits[3], (N_DP, CAP), ((0, 2),), -0.2, 0.2)), 0.1, 1.0)
    w_gate = normal_values(streams_of[4], (D, FF), D ** -0.5, 0.125, ((0, 2), (1, 8)))
    w_up = normal_values(streams_of[5], (D, FF), D ** -0.5, 0.125, ((0, 2), (1, 8)))
    w_down = normal_values(streams_of[6], (FF, D), FF ** -0.5, 0.125, ((0, 8), (1, 2)))
    return dict(tokens=tokens, grad_out=grad_out, picks=picks, scores=scores, w_gate=w_gate, w_up=w_up, w_down=w_down)


def reference(tokens, grad_out, picks, scores, w_gate, w_up, w_down):
    coeff = float(N_DP * CAP) ** -0.5
    grad_rows = []
    total_gate = jnp.zeros(w_gate.shape, jnp.float32)
    total_up = jnp.zeros(w_up.shape, jnp.float32)
    total_down = jnp.zeros(w_down.shape, jnp.float32)
    for replica in range(N_DP):
        chosen = picks[replica].astype(jnp.int32)
        x_rows = jnp.take(tokens[replica], chosen, axis=0)
        dy_rows = jnp.take(grad_out[replica], chosen, axis=0)
        dz = (scores[replica][:, None] * dy_rows.astype(jnp.float32)).astype(jnp.bfloat16)
        gate = jnp.dot(x_rows, w_gate, preferred_element_type=jnp.float32)
        upper = jnp.dot(x_rows, w_up, preferred_element_type=jnp.float32)
        sigma = jax.nn.sigmoid(gate)
        act = (gate * sigma * upper).astype(jnp.bfloat16)
        d_act = jnp.dot(dz, w_down.T, preferred_element_type=jnp.float32)
        d_gate = (d_act * upper * sigma * (1.0 + gate * (1.0 - sigma))).astype(jnp.bfloat16)
        d_up = (d_act * gate * sigma).astype(jnp.bfloat16)
        dx = jnp.dot(d_gate, w_gate.T, preferred_element_type=jnp.float32)
        dx = dx + jnp.dot(d_up, w_up.T, preferred_element_type=jnp.float32)
        full = jnp.zeros((tokens.shape[1], tokens.shape[2]), jnp.bfloat16)
        grad_rows.append(full.at[chosen].set(dx.astype(jnp.bfloat16)))
        term_gate = (coeff * jnp.dot(x_rows.T, d_gate, preferred_element_type=jnp.float32)).astype(jnp.bfloat16)
        term_up = (coeff * jnp.dot(x_rows.T, d_up, preferred_element_type=jnp.float32)).astype(jnp.bfloat16)
        term_down = (coeff * jnp.dot(act.T, dz, preferred_element_type=jnp.float32)).astype(jnp.bfloat16)
        term_gate, term_up, term_down = lax.optimization_barrier((term_gate, term_up, term_down))
        total_gate = total_gate + term_gate.astype(jnp.float32)
        total_up = total_up + term_up.astype(jnp.float32)
        total_down = total_down + term_down.astype(jnp.float32)
    grad_tokens = jnp.stack(grad_rows, axis=0)
    return (grad_tokens, total_gate.astype(jnp.bfloat16), total_up.astype(jnp.bfloat16), total_down.astype(jnp.bfloat16))
```

```python
import functools

import jax
import jax.numpy as jnp
from jax import lax
from jax.experimental import pallas as pl
from jax.experimental.pallas import tpu as pltpu
from jax.sharding import PartitionSpec as P

MOST = 32
BF = jnp.bfloat16
F32 = jnp.float32
NN = (((1,), (0,)), ((), ()))
NT = (((1,), (1,)), ((), ()))
TN = (((0,), (0,)), ((), ()))


def dot(a, b, dims):
    return lax.dot_general(a, b, dims, preferred_element_type=F32)


def call(body, outs, *args, flops=0):
    size = sum(a.size * a.dtype.itemsize for a in args) + sum(o.size * o.dtype.itemsize for o in outs)
    return pl.pallas_call(
        body,
        out_shape=outs,
        in_specs=[pl.BlockSpec(memory_space=pltpu.VMEM)] * len(args),
        out_specs=[pl.BlockSpec(memory_space=pltpu.VMEM)] * len(outs),
        cost_estimate=pl.CostEstimate(flops=flops, bytes_accessed=size, transcendentals=0),
        compiler_params=pltpu.CompilerParams(vmem_limit_bytes=24 * 1024 * 1024),
    )(*args)


def arr(shape, dtype=BF):
    return jax.ShapeDtypeStruct(shape, dtype)


def pack_body(picks_ref, scores_ref, tok_ref, grad_ref, x_ref, dz_ref, sel_ref):
    tok_dev = tok_ref.shape[0]
    cap = picks_ref.shape[1]
    base = lax.axis_index("seq") * tok_dev
    where = picks_ref[...] - base
    hit = (lax.broadcasted_iota(jnp.int32, (tok_dev, cap), 0) == where).astype(F32).astype(BF)
    picked = dot(jnp.ones((8, cap), BF), hit, NT)
    before = (
        lax.broadcasted_iota(jnp.int32, (tok_dev, tok_dev), 0) < lax.broadcasted_iota(jnp.int32, (tok_dev, tok_dev), 1)
    ).astype(F32).astype(BF)
    rank = dot(picked.astype(BF), before, NN)[0:1]
    slots = lax.broadcasted_iota(jnp.int32, (MOST, tok_dev), 0).astype(F32)
    sel = jnp.where((rank == slots) & (picked[0:1] > 0.5), 1.0, 0.0).astype(BF)
    sel_ref[...] = sel
    chosen = dot(sel, hit, NN)
    score = jnp.sum(chosen * scores_ref[...], axis=1, keepdims=True)
    x_ref[...] = dot(sel, tok_ref[...], NN).astype(BF)
    dz_ref[...] = (score * dot(sel, grad_ref[...], NN)).astype(BF)


def rows_of(refs):
    return jnp.concatenate([r[...] for r in refs], axis=0)


def gate_up_body(n, *refs):
    x = rows_of(refs[:n])
    gate_own, gate_oth, up_own, up_oth, send_ref, keep_ref = refs[n:]
    h = gate_own.shape[0]
    for i, w in enumerate((gate_own, gate_oth, up_own, up_oth)):
        part = dot(w[...], x, NT)
        keep_ref[i * h : (i + 1) * h] = part
        send_ref[i * h : (i + 1) * h] = part.astype(BF)


def d_act_body(n, *refs):
    dz = rows_of(refs[:n])
    down_own, down_oth, send_ref, keep_ref = refs[n:]
    h = down_own.shape[0]
    for i, w in enumerate((down_own, down_oth)):
        part = dot(w[...], dz, NT)
        keep_ref[i * h : (i + 1) * h] = part
        send_ref[i * h : (i + 1) * h] = part.astype(BF)


def middle_body(n, gu_keep, gu_recv, da_keep, da_recv, gate_own, gate_oth, up_own, up_oth, own_ref, oth_ref, *dx_refs):
    h = gate_own.shape[0]
    total = jnp.zeros((gu_keep.shape[1], gate_own.shape[1]), F32)
    for i, (wg, wu, out) in enumerate(((gate_own, up_own, own_ref), (gate_oth, up_oth, oth_ref))):
        at = slice(i * h, (i + 1) * h)
        au = slice((2 + i) * h, (3 + i) * h)
        gate = gu_keep[at] + gu_recv[at].astype(F32)
        upper = gu_keep[au] + gu_recv[au].astype(F32)
        d_act = da_keep[at] + da_recv[at].astype(F32)
        sigma = jax.nn.sigmoid(gate)
        gs = gate * sigma
        d_gate = (d_act * upper * sigma * (1.0 + gate * (1.0 - sigma))).astype(BF)
        d_up = (d_act * gs).astype(BF)
        out[0:h] = d_gate
        out[h : 2 * h] = d_up
        out[2 * h : 3 * h] = (gs * upper).astype(BF)
        total += dot(d_gate, wg[...], TN) + dot(d_up, wu[...], TN)
    for s, ref in enumerate(dx_refs):
        ref[...] = total[s * MOST : (s + 1) * MOST].astype(BF)


def weights_body(n, coeff, h, *refs):
    x_own, x_oth, dz_own, dz_oth = (rows_of(refs[i * n : (i + 1) * n]) for i in range(4))
    own, oth, gate_ref, up_ref, down_ref = refs[4 * n :]
    for i, (a, b, out) in enumerate(((x_own, x_oth, gate_ref), (x_own, x_oth, up_ref), (dz_own, dz_oth, down_ref))):
        at = slice(i * h, (i + 1) * h)
        one = (coeff * dot(own[at], a, NN)).astype(BF).astype(F32)
        two = (coeff * dot(oth[at], b, NN)).astype(BF).astype(F32)
        out[...] = (one + two).astype(BF)


def spread_body(sel_ref, *refs):
    total = refs[0][...].astype(F32)
    for r in refs[1:-1]:
        total += r[...].astype(F32)
    refs[-1][...] = dot(sel_ref[...], total.astype(BF), TN).astype(BF)


def swapped(tokens, grad_out, picks, scores, w_gate, w_up, w_down):
    n = lax.axis_size("seq")
    replicas = lax.axis_size("dp")
    tok_dev, half = tokens.shape[1:]
    cap = picks.shape[1]
    h = w_gate.shape[1]
    rows = n * MOST
    coeff = float(replicas * cap) ** -0.5

    def index(d, k, t):
        return (k * 2 + d) * 2 + t

    def across(x, s):
        pairs = [(index(d, k, t), index(t, k ^ s, d)) for d in range(2) for k in range(n) for t in range(2)]
        return lax.ppermute(x, ("seq", "dp", "tensor"), pairs)

    def swap(x, axis):
        return lax.ppermute(x, axis, [(0, 1), (1, 0)])

    gate, up, down = w_gate.T, w_up.T, w_down
    x_mine, dz_mine, sel = call(
        pack_body,
        [arr((MOST, half)), arr((MOST, half)), arr((MOST, tok_dev))],
        picks, scores, tokens[0], grad_out[0],
    )
    order = range(n)
    x_own = [across(x_mine, s) for s in order]
    dz_own = [across(dz_mine, s) for s in order]
    gate_oth, up_oth, down_oth = (swap(w, "tensor") for w in (gate, up, down))
    flops = 2 * rows * half * h
    gu_send, gu_keep = call(
        functools.partial(gate_up_body, n), [arr((4 * h, rows)), arr((4 * h, rows), F32)],
        *x_own, gate, gate_oth, up, up_oth, flops=4 * flops,
    )
    gu_recv = swap(gu_send, "dp")
    da_send, da_keep = call(
        functools.partial(d_act_body, n), [arr((2 * h, rows)), arr((2 * h, rows), F32)],
        *dz_own, down, down_oth, flops=2 * flops,
    )
    da_recv = swap(da_send, "dp")
    x_oth = [swap(b, "tensor") for b in x_own]
    dz_oth = [swap(b, "tensor") for b in dz_own]
    own, lent, *dx = call(
        functools.partial(middle_body, n),
        [arr((3 * h, rows))] * 2 + [arr((MOST, half))] * n,
        gu_keep, gu_recv, da_keep, da_recv, gate, gate_oth, up, up_oth, flops=4 * flops,
    )
    back = [across(b, s) for s, b in enumerate(dx)]
    oth = swap(lent, "tensor")
    grads = call(
        functools.partial(weights_body, n, coeff, h), [arr((h, half))] * 3,
        *x_own, *x_oth, *dz_own, *dz_oth, own, oth, flops=6 * flops,
    )
    (grad_local,) = call(spread_body, [arr((tok_dev, half))], sel, *back)
    return grad_local[None], grads[0].T, grads[1].T, grads[2]


def gathered(tokens, grad_out, picks, scores, w_gate, w_up, w_down):
    tok_dev = tokens.shape[1]
    half = tokens.shape[2]
    seq_count = lax.axis_size("seq")
    ten_count = lax.axis_size("tensor")
    picks_row = picks[0]
    score_row = scores[0]
    cap = picks_row.shape[0]
    each = cap // (seq_count * ten_count)
    my_seq = lax.axis_index("seq")
    my_ten = lax.axis_index("tensor")
    my_replica = lax.axis_index("dp")
    share = w_gate.shape[0]
    full_gate, full_up, full_down = (
        lax.all_gather(w_gate, "dp", axis=0, tiled=True),
        lax.all_gather(w_up, "dp", axis=0, tiled=True),
        lax.all_gather(w_down, "dp", axis=1, tiled=True),
    )
    owner = picks_row // tok_dev
    mine = owner == my_seq
    place = jnp.clip(picks_row - my_seq * tok_dev, 0, tok_dev - 1)
    local_rows = tokens[0]
    local_grads = grad_out[0]
    zero_value = jnp.zeros((), jnp.bfloat16)
    shard_ids = jnp.arange(seq_count, dtype=jnp.int32)
    owner_table = (owner[:, None] == shard_ids[None, :]).astype(jnp.int32)
    earlier = jnp.cumsum(owner_table, axis=0) - owner_table
    slot_of = jnp.sum(earlier * owner_table, axis=1)
    slot_ids = jnp.arange(MOST, dtype=jnp.int32)
    match = (mine[None, :] & (slot_of[None, :] == slot_ids[:, None])).astype(jnp.int32)
    pick_ids = jnp.sum(match * jnp.arange(cap, dtype=jnp.int32)[None, :], axis=1)
    valid = jnp.sum(match, axis=1) > 0
    rows_at = jnp.clip(jnp.take(picks_row, pick_ids) - my_seq * tok_dev, 0, tok_dev - 1)
    pack_rows = jnp.where(valid[:, None], jnp.take(local_rows, rows_at, axis=0), zero_value)
    pack_grads = jnp.where(valid[:, None], jnp.take(local_grads, rows_at, axis=0), zero_value)
    all_rows, all_grads = (
        lax.all_gather(pack_rows, ("seq", "tensor"), axis=0, tiled=True),
        lax.all_gather(pack_grads, ("seq", "tensor"), axis=0, tiled=True),
    )

    def unpack(block):
        parts = [
            jnp.take(block, (owner * ten_count + part) * MOST + slot_of, axis=0)
            for part in range(ten_count)
        ]
        return jnp.concatenate(parts, axis=1)

    x_rows = unpack(all_rows)
    dy_rows = unpack(all_grads)
    dz = (score_row[:, None] * dy_rows.astype(jnp.float32)).astype(jnp.bfloat16)
    gate = jnp.dot(x_rows, full_gate, preferred_element_type=jnp.float32)
    upper = jnp.dot(x_rows, full_up, preferred_element_type=jnp.float32)
    sigma = jax.nn.sigmoid(gate)
    act = (gate * sigma * upper).astype(jnp.bfloat16)
    last_dims = (((1,), (1,)), ((), ()))
    first_dims = (((0,), (0,)), ((), ()))
    d_act = lax.dot_general(dz, full_down, last_dims, preferred_element_type=jnp.float32)
    d_gate = (d_act * upper * sigma * (1.0 + gate * (1.0 - sigma))).astype(jnp.bfloat16)
    d_up = (d_act * gate * sigma).astype(jnp.bfloat16)
    result = lax.dot_general(d_gate, full_gate, last_dims, preferred_element_type=jnp.float32)
    summed = lax.psum_scatter(
        result + lax.dot_general(d_up, full_up, last_dims, preferred_element_type=jnp.float32),
        ("seq", "tensor"),
        scatter_dimension=0,
        tiled=True,
    )
    coeff = float(lax.axis_size("dp") * cap) ** (-0.5)
    term_gate = (
        coeff * lax.dot_general(x_rows, d_gate, first_dims, preferred_element_type=jnp.float32)
    ).astype(jnp.bfloat16)
    term_up = (
        coeff * lax.dot_general(x_rows, d_up, first_dims, preferred_element_type=jnp.float32)
    ).astype(jnp.bfloat16)
    term_down = (
        coeff * lax.dot_general(act, dz, first_dims, preferred_element_type=jnp.float32)
    ).astype(jnp.bfloat16)
    sum_gate, sum_up, sum_down = (
        lax.psum(term_gate, "dp").astype(jnp.float32),
        lax.psum(term_up, "dp").astype(jnp.float32),
        lax.psum(term_down, "dp").astype(jnp.float32),
    )
    own_gate = lax.dynamic_slice_in_dim(sum_gate, my_replica * share, share, 0)
    own_up = lax.dynamic_slice_in_dim(sum_up, my_replica * share, share, 0)
    own_down = lax.dynamic_slice_in_dim(sum_down, my_replica * share, share, 1)
    my_block = my_seq * ten_count + my_ten
    block_owner = lax.dynamic_slice_in_dim(owner, my_block * each, each, 0)
    block_rows = summed.astype(jnp.bfloat16).reshape(each, ten_count, half).transpose(1, 0, 2)
    targets = block_owner[None, :] == jnp.arange(seq_count, dtype=jnp.int32)[:, None]
    outgoing = jnp.where(targets[:, None, :, None], block_rows[None], zero_value)
    incoming = lax.all_to_all(
        outgoing.reshape(seq_count * ten_count * each, half),
        ("seq", "tensor"),
        split_axis=0,
        concat_axis=0,
        tiled=True,
    )
    positions = jnp.arange(tok_dev, dtype=jnp.int32)
    selector = ((place[None, :] == positions[:, None]) & mine[None, :]).astype(jnp.bfloat16)
    grad_local = jnp.dot(selector, incoming, preferred_element_type=jnp.float32).astype(
        jnp.bfloat16
    )
    return (
        grad_local.reshape(1, tok_dev, half),
        own_gate.astype(jnp.bfloat16),
        own_up.astype(jnp.bfloat16),
        own_down.astype(jnp.bfloat16),
    )


def solution(mesh):
    in_specs = (
        P(("groups", "dp"), "seq", "tensor"),
        P(("groups", "dp"), "seq", "tensor"),
        P(("groups", "dp"), None),
        P(("groups", "dp"), None),
        P("dp", ("seq", "tensor")),
        P("dp", ("seq", "tensor")),
        P(("seq", "tensor"), "dp"),
    )
    out_specs = (
        P(("groups", "dp"), "seq", "tensor"),
        P(("groups", "dp"), ("seq", "tensor")),
        P(("groups", "dp"), ("seq", "tensor")),
        P(("groups", "seq", "tensor"), "dp"),
    )
    size = mesh.shape
    pairs = size["dp"] == size["tensor"] == 2 and size["seq"] in (2, 4, 8)
    local = swapped if pairs else gathered
    return jax.shard_map(local, mesh=mesh, in_specs=in_specs, out_specs=out_specs, check_vma=False)
```

```python
import functools

import jax
import jax.numpy as jnp
from jax import lax
from jax.experimental import pallas as pl
from jax.experimental.pallas import tpu as pltpu
from jax.sharding import PartitionSpec as P

MOST = 32
BF = jnp.bfloat16
F32 = jnp.float32
NN = (((1,), (0,)), ((), ()))
NT = (((1,), (1,)), ((), ()))
TN = (((0,), (0,)), ((), ()))


def dot(a, b, dims):
    return lax.dot_general(a, b, dims, preferred_element_type=F32)


def call(body, outs, *args, flops=0, after=(), far=False, scratch=(), mib=24, far_out=0):
    size = sum(a.size * a.dtype.itemsize for a in args) + sum(o.size * o.dtype.itemsize for o in outs)
    count = len(args)

    def run(*refs):
        body(*refs[:count], *refs[count + len(after) :])

    return pl.pallas_call(
        run,
        out_shape=outs,
        in_specs=[pl.BlockSpec(memory_space=pltpu.HBM if far else pltpu.VMEM)] * len(args)
        + [pl.BlockSpec(memory_space=pl.ANY)] * len(after),
        out_specs=[pl.BlockSpec(memory_space=pltpu.VMEM)] * (len(outs) - far_out) + [pl.BlockSpec(memory_space=pltpu.HBM)] * far_out,
        scratch_shapes=list(scratch),
        cost_estimate=pl.CostEstimate(flops=flops, bytes_accessed=size, transcendentals=0),
        compiler_params=pltpu.CompilerParams(vmem_limit_bytes=int(mib * 1024 * 1024)),
    )(*args, *after)


def arr(shape, dtype=BF):
    return jax.ShapeDtypeStruct(shape, dtype)


def pack_body(picks_in, scores_in, tok_in, grad_in, gate_in, up_in, down_in, xd_ref, sel_ref, w_out, picks_ref, scores_ref, tok_ref, grad_ref, w_ref, sems):
    pairs = [(picks_in, picks_ref), (scores_in, scores_ref), (tok_in, tok_ref), (grad_in, grad_ref)]
    h = gate_in.shape[0]
    pairs += [(w, w_ref.at[i * h : (i + 1) * h]) for i, w in enumerate((gate_in, up_in, down_in))]
    copies = [pltpu.make_async_copy(a, b, sems.at[i]) for i, (a, b) in enumerate(pairs)]
    for c in copies:
        c.start()
    tok_dev = tok_ref.shape[0]
    cap = picks_ref.shape[1]
    base = lax.axis_index("seq") * tok_dev
    before = (
        lax.broadcasted_iota(jnp.int32, (tok_dev, tok_dev), 0) < lax.broadcasted_iota(jnp.int32, (tok_dev, tok_dev), 1)
    ).astype(F32).astype(BF)
    slots = lax.broadcasted_iota(jnp.int32, (MOST, tok_dev), 0).astype(F32)
    copies[0].wait()
    where = picks_ref[...] - base
    hit = (lax.broadcasted_iota(jnp.int32, (tok_dev, cap), 0) == where).astype(F32).astype(BF)
    picked = dot(jnp.ones((8, cap), BF), hit, NT)
    rank = dot(picked.astype(BF), before, NN)[0:1]
    sel = jnp.where((rank == slots) & (picked[0:1] > 0.5), 1.0, 0.0).astype(BF)
    sel_ref[...] = sel
    chosen = dot(sel, hit, NN)
    for c in copies[4:]:
        c.wait()
    out = pltpu.make_async_copy(w_ref, w_out, sems.at[7])
    out.start()
    copies[1].wait()
    score = jnp.sum(chosen * scores_ref[...], axis=1, keepdims=True)
    copies[2].wait()
    xd_ref[0:MOST] = dot(sel, tok_ref[...], NN).astype(BF)
    copies[3].wait()
    xd_ref[MOST:] = (score * dot(sel, grad_ref[...], NN)).astype(BF)
    out.wait()


def partial_body(blocks, *refs):
    w_own, w_oth, keep_ref = refs[blocks : blocks + 3]
    h = w_own.shape[0] // 3
    x = jnp.concatenate([r[0:MOST] for r in refs[:blocks]], axis=0)
    dz = jnp.concatenate([r[MOST:] for r in refs[:blocks]], axis=0)
    for at, a in ((slice(0, 2 * h), x), (slice(2 * h, 3 * h), dz)):
        keep_ref[at] = jnp.concatenate([dot(w[at], a, NT) for w in (w_own, w_oth)], axis=1)
    done = 0
    for send_ref in refs[blocks + 3 :]:
        send_ref[...] = keep_ref[done : done + send_ref.shape[0]].astype(BF)
        done += send_ref.shape[0]


def terms(keep, recv, dd_ref):
    h = keep.shape[0] // 3
    got = jnp.concatenate([r[...] for r in recv], axis=0).astype(F32)
    gate, upper, d_act = (keep[i * h : (i + 1) * h] + got[i * h : (i + 1) * h] for i in range(3))
    sigma = jax.nn.sigmoid(gate)
    gs = gate * sigma
    dd_ref[0:h] = (d_act * upper * sigma * (1.0 + gate * (1.0 - sigma))).astype(BF)
    dd_ref[h : 2 * h] = (d_act * gs).astype(BF)
    dd_ref[2 * h :] = (gs * upper).astype(BF)


def back_rows(dd, w_own, w_oth, dx_refs):
    at = slice(0, 2 * w_own.shape[0] // 3)
    m = dd.shape[1] // 2
    total = dot(dd[at], w_own[at], TN)[0:m] + dot(dd[at], w_oth[at], TN)[m:]
    for s, ref in enumerate(dx_refs):
        ref[...] = total[s * MOST : (s + 1) * MOST].astype(BF)


def first_body(recv, keep, *refs):
    w_own, w_oth, dd_ref, *dx_refs = refs[recv:]
    terms(keep, refs[:recv], dd_ref)
    back_rows(dd_ref, w_own, w_oth, dx_refs)


def second_body(blocks, keep, recv, w_own, w_oth, dd_a, *refs):
    dd_ref, rows_ref, *dx_refs = refs[blocks:]
    m = dd_a.shape[1]
    terms(keep, [recv], dd_ref.at[:, m:])
    back_rows(dd_ref.at[:, m:], w_own, w_oth, dx_refs)
    dd_ref[:, 0:m] = dd_a[...]
    for s, block in enumerate(refs[:blocks]):
        rows_ref[s * MOST : (s + 1) * MOST] = block[0:MOST]
        rows_ref[(blocks + s) * MOST : (blocks + s + 1) * MOST] = block[MOST:]


def weights_body(coeff, rows_own, rows_oth, own, oth, gate_ref, up_ref, down_ref, token_ref):
    h = gate_ref.shape[0]
    m = rows_own.shape[0] // 4
    zero = jnp.zeros((m, rows_own.shape[1]), BF)
    for i, out in enumerate((gate_ref, up_ref, down_ref)):
        at = slice(i * h, (i + 1) * h)
        r = 0 if i < 2 else 2 * m
        mine = jnp.concatenate([rows_own[r : r + m], zero, rows_own[r + m : r + 2 * m], zero], axis=0)
        others = jnp.concatenate([zero, rows_oth[r : r + m], zero, rows_oth[r + m : r + 2 * m]], axis=0)
        one = dot(own[at], mine, NN)
        two = dot(oth[at], others, NN)
        out[...] = ((coeff * one).astype(BF).astype(F32) + (coeff * two).astype(BF).astype(F32)).astype(BF)
    token_ref[...] = jnp.zeros_like(token_ref)


def spread_body(sel_ref, *refs):
    total = refs[0][...].astype(F32)
    for r in refs[1:-1]:
        total += r[...].astype(F32)
    refs[-1][...] = dot(sel_ref[...], total.astype(BF), TN).astype(BF)


def swapped(tokens, grad_out, picks, scores, w_gate, w_up, w_down):
    n = lax.axis_size("seq")
    replicas = lax.axis_size("dp")
    tok_dev, half = tokens.shape[1:]
    cap = picks.shape[1]
    h = w_gate.shape[1]
    m = n // 2 * MOST
    coeff = float(replicas * cap) ** -0.5

    def index(d, k, t):
        return (k * 2 + d) * 2 + t

    def across(x, s):
        pairs = [(index(d, k, t), index(t, k ^ s, d)) for d in range(2) for k in range(n) for t in range(2)]
        return lax.ppermute(x, ("seq", "dp", "tensor"), pairs)

    def swap(x, axis):
        return lax.ppermute(x, axis, [(0, 1), (1, 0)])

    xd, sel, w_own = call(
        pack_body,
        [arr((2 * MOST, half)), arr((MOST, tok_dev)), arr((3 * h, half))],
        picks, scores, tokens[0], grad_out[0], w_gate.T, w_up.T, w_down,
        far=True, far_out=1, mib=60,
        scratch=[pltpu.VMEM((1, cap), jnp.int32), pltpu.VMEM((1, cap), F32), pltpu.VMEM((tok_dev, half), BF),
                 pltpu.VMEM((tok_dev, half), BF), pltpu.VMEM((3 * h, half), BF), pltpu.SemaphoreType.DMA((8,))],
    )
    blocks = {s: across(xd, s) for s in range(n)}
    w_oth = swap(w_own, "tensor")
    flops = 2 * m * half * h

    def partial(group, parts, after=()):
        keep, *send = call(
            functools.partial(partial_body, len(group)),
            [arr((3 * h, 2 * m), F32)] + [arr((p * h, 2 * m)) for p in parts],
            *(blocks[s] for s in group), w_own, w_oth, flops=6 * flops, after=after,
        )
        return keep, [swap(b, "dp") for b in send]

    near, far = range(n // 2), range(n // 2, n)
    dx = [arr((MOST, half))] * (n // 2)
    keep_a, recv_a = partial(near, (2, 1))
    keep_b, recv_b = partial(far, (3,), after=recv_a)
    dd_a, *dx_a = call(
        functools.partial(first_body, len(recv_a)), [arr((3 * h, 2 * m))] + dx,
        keep_a, *recv_a, w_own, w_oth, flops=8 * flops, after=(keep_b,),
    )
    back = [across(b, s) for s, b in zip(near, dx_a)]
    own, rows_own, *dx_b = call(
        functools.partial(second_body, n), [arr((3 * h, 4 * m)), arr((2 * n * MOST, half))] + dx,
        keep_b, *recv_b, w_own, w_oth, dd_a, *(blocks[s] for s in range(n)), flops=8 * flops, after=back,
    )
    back += [across(b, s) for s, b in zip(far, dx_b)]
    rows_oth, oth = swap(rows_own, "tensor"), swap(own, "tensor")
    grads = call(
        functools.partial(weights_body, coeff), [arr((h, half))] * 3 + [arr((8, 128), F32)],
        rows_own, rows_oth, own, oth, flops=12 * flops,
    )
    (grad_local,) = call(spread_body, [arr((tok_dev, half))], sel, *back, after=grads[3:])
    return grad_local[None], grads[0].T, grads[1].T, grads[2]


def gathered(tokens, grad_out, picks, scores, w_gate, w_up, w_down):
    tok_dev = tokens.shape[1]
    half = tokens.shape[2]
    seq_count = lax.axis_size("seq")
    ten_count = lax.axis_size("tensor")
    picks_row = picks[0]
    score_row = scores[0]
    cap = picks_row.shape[0]
    each = cap // (seq_count * ten_count)
    my_seq = lax.axis_index("seq")
    my_ten = lax.axis_index("tensor")
    my_replica = lax.axis_index("dp")
    share = w_gate.shape[0]
    full_gate, full_up, full_down = (
        lax.all_gather(w_gate, "dp", axis=0, tiled=True),
        lax.all_gather(w_up, "dp", axis=0, tiled=True),
        lax.all_gather(w_down, "dp", axis=1, tiled=True),
    )
    owner = picks_row // tok_dev
    mine = owner == my_seq
    place = jnp.clip(picks_row - my_seq * tok_dev, 0, tok_dev - 1)
    local_rows = tokens[0]
    local_grads = grad_out[0]
    zero_value = jnp.zeros((), jnp.bfloat16)
    shard_ids = jnp.arange(seq_count, dtype=jnp.int32)
    owner_table = (owner[:, None] == shard_ids[None, :]).astype(jnp.int32)
    earlier = jnp.cumsum(owner_table, axis=0) - owner_table
    slot_of = jnp.sum(earlier * owner_table, axis=1)
    slot_ids = jnp.arange(MOST, dtype=jnp.int32)
    match = (mine[None, :] & (slot_of[None, :] == slot_ids[:, None])).astype(jnp.int32)
    pick_ids = jnp.sum(match * jnp.arange(cap, dtype=jnp.int32)[None, :], axis=1)
    valid = jnp.sum(match, axis=1) > 0
    rows_at = jnp.clip(jnp.take(picks_row, pick_ids) - my_seq * tok_dev, 0, tok_dev - 1)
    pack_rows = jnp.where(valid[:, None], jnp.take(local_rows, rows_at, axis=0), zero_value)
    pack_grads = jnp.where(valid[:, None], jnp.take(local_grads, rows_at, axis=0), zero_value)
    all_rows, all_grads = (
        lax.all_gather(pack_rows, ("seq", "tensor"), axis=0, tiled=True),
        lax.all_gather(pack_grads, ("seq", "tensor"), axis=0, tiled=True),
    )

    def unpack(block):
        parts = [
            jnp.take(block, (owner * ten_count + part) * MOST + slot_of, axis=0)
            for part in range(ten_count)
        ]
        return jnp.concatenate(parts, axis=1)

    x_rows = unpack(all_rows)
    dy_rows = unpack(all_grads)
    dz = (score_row[:, None] * dy_rows.astype(jnp.float32)).astype(jnp.bfloat16)
    gate = jnp.dot(x_rows, full_gate, preferred_element_type=jnp.float32)
    upper = jnp.dot(x_rows, full_up, preferred_element_type=jnp.float32)
    sigma = jax.nn.sigmoid(gate)
    act = (gate * sigma * upper).astype(jnp.bfloat16)
    last_dims = (((1,), (1,)), ((), ()))
    first_dims = (((0,), (0,)), ((), ()))
    d_act = lax.dot_general(dz, full_down, last_dims, preferred_element_type=jnp.float32)
    d_gate = (d_act * upper * sigma * (1.0 + gate * (1.0 - sigma))).astype(jnp.bfloat16)
    d_up = (d_act * gate * sigma).astype(jnp.bfloat16)
    result = lax.dot_general(d_gate, full_gate, last_dims, preferred_element_type=jnp.float32)
    summed = lax.psum_scatter(
        result + lax.dot_general(d_up, full_up, last_dims, preferred_element_type=jnp.float32),
        ("seq", "tensor"),
        scatter_dimension=0,
        tiled=True,
    )
    coeff = float(lax.axis_size("dp") * cap) ** (-0.5)
    term_gate = (
        coeff * lax.dot_general(x_rows, d_gate, first_dims, preferred_element_type=jnp.float32)
    ).astype(jnp.bfloat16)
    term_up = (
        coeff * lax.dot_general(x_rows, d_up, first_dims, preferred_element_type=jnp.float32)
    ).astype(jnp.bfloat16)
    term_down = (
        coeff * lax.dot_general(act, dz, first_dims, preferred_element_type=jnp.float32)
    ).astype(jnp.bfloat16)
    sum_gate, sum_up, sum_down = (
        lax.psum(term_gate, "dp").astype(jnp.float32),
        lax.psum(term_up, "dp").astype(jnp.float32),
        lax.psum(term_down, "dp").astype(jnp.float32),
    )
    own_gate = lax.dynamic_slice_in_dim(sum_gate, my_replica * share, share, 0)
    own_up = lax.dynamic_slice_in_dim(sum_up, my_replica * share, share, 0)
    own_down = lax.dynamic_slice_in_dim(sum_down, my_replica * share, share, 1)
    my_block = my_seq * ten_count + my_ten
    block_owner = lax.dynamic_slice_in_dim(owner, my_block * each, each, 0)
    block_rows = summed.astype(jnp.bfloat16).reshape(each, ten_count, half).transpose(1, 0, 2)
    targets = block_owner[None, :] == jnp.arange(seq_count, dtype=jnp.int32)[:, None]
    outgoing = jnp.where(targets[:, None, :, None], block_rows[None], zero_value)
    incoming = lax.all_to_all(
        outgoing.reshape(seq_count * ten_count * each, half),
        ("seq", "tensor"),
        split_axis=0,
        concat_axis=0,
        tiled=True,
    )
    positions = jnp.arange(tok_dev, dtype=jnp.int32)
    selector = ((place[None, :] == positions[:, None]) & mine[None, :]).astype(jnp.bfloat16)
    grad_local = jnp.dot(selector, incoming, preferred_element_type=jnp.float32).astype(
        jnp.bfloat16
    )
    return (
        grad_local.reshape(1, tok_dev, half),
        own_gate.astype(jnp.bfloat16),
        own_up.astype(jnp.bfloat16),
        own_down.astype(jnp.bfloat16),
    )


def solution(mesh):
    in_specs = (
        P(("groups", "dp"), "seq", "tensor"),
        P(("groups", "dp"), "seq", "tensor"),
        P(("groups", "dp"), None),
        P(("groups", "dp"), None),
        P("dp", ("seq", "tensor")),
        P("dp", ("seq", "tensor")),
        P(("seq", "tensor"), "dp"),
    )
    out_specs = (
        P(("groups", "dp"), "seq", "tensor"),
        P(("groups", "dp"), ("seq", "tensor")),
        P(("groups", "dp"), ("seq", "tensor")),
        P(("groups", "seq", "tensor"), "dp"),
    )
    size = mesh.shape
    pairs = size["dp"] == size["tensor"] == 2 and size["seq"] in (2, 4, 8)
    local = swapped if pairs else gathered
    return jax.shard_map(local, mesh=mesh, in_specs=in_specs, out_specs=out_specs, check_vma=False)
```

```python
import functools

import jax
import jax.numpy as jnp
from jax import lax
from jax.experimental import pallas as pl
from jax.experimental.pallas import tpu as pltpu
from jax.sharding import PartitionSpec as P

MOST = 32
BF = jnp.bfloat16
F32 = jnp.float32
NN = (((1,), (0,)), ((), ()))
NT = (((1,), (1,)), ((), ()))
TN = (((0,), (0,)), ((), ()))


def dot(a, b, dims):
    return lax.dot_general(a, b, dims, preferred_element_type=F32)


def call(body, outs, *args, flops=0, after=(), far=False, scratch=(), mib=24, far_out=0):
    size = sum(a.size * a.dtype.itemsize for a in args) + sum(o.size * o.dtype.itemsize for o in outs)
    count = len(args)

    def run(*refs):
        body(*refs[:count], *refs[count + len(after) :])

    return pl.pallas_call(
        run,
        out_shape=outs,
        in_specs=[pl.BlockSpec(memory_space=pltpu.HBM if far else pltpu.VMEM)] * len(args)
        + [pl.BlockSpec(memory_space=pl.ANY)] * len(after),
        out_specs=[pl.BlockSpec(memory_space=pltpu.VMEM)] * (len(outs) - far_out) + [pl.BlockSpec(memory_space=pltpu.HBM)] * far_out,
        scratch_shapes=list(scratch),
        cost_estimate=pl.CostEstimate(flops=flops, bytes_accessed=size, transcendentals=0),
        compiler_params=pltpu.CompilerParams(vmem_limit_bytes=int(mib * 1024 * 1024)),
    )(*args, *after)


def arr(shape, dtype=BF):
    return jax.ShapeDtypeStruct(shape, dtype)


def pack_body(picks_in, scores_in, tok_in, grad_in, gate_in, up_in, down_in, xd_ref, sel_ref, w_out, picks_ref, scores_ref, tok_ref, grad_ref, w_ref, sems):
    pairs = [(picks_in, picks_ref), (scores_in, scores_ref), (tok_in, tok_ref), (grad_in, grad_ref)]
    h = gate_in.shape[0]
    pairs += [(w, w_ref.at[i * h : (i + 1) * h]) for i, w in enumerate((gate_in, up_in, down_in))]
    copies = [pltpu.make_async_copy(a, b, sems.at[i]) for i, (a, b) in enumerate(pairs)]
    for c in copies:
        c.start()
    tok_dev = tok_ref.shape[0]
    cap = picks_ref.shape[1]
    base = lax.axis_index("seq") * tok_dev
    before = (
        lax.broadcasted_iota(jnp.int32, (tok_dev, tok_dev), 0) < lax.broadcasted_iota(jnp.int32, (tok_dev, tok_dev), 1)
    ).astype(F32).astype(BF)
    slots = lax.broadcasted_iota(jnp.int32, (MOST, tok_dev), 0).astype(F32)
    copies[0].wait()
    where = picks_ref[...] - base
    hit = (lax.broadcasted_iota(jnp.int32, (tok_dev, cap), 0) == where).astype(F32).astype(BF)
    picked = dot(jnp.ones((8, cap), BF), hit, NT)
    rank = dot(picked.astype(BF), before, NN)[0:1]
    sel = jnp.where((rank == slots) & (picked[0:1] > 0.5), 1.0, 0.0).astype(BF)
    sel_ref[...] = sel
    chosen = dot(sel, hit, NN)
    for c in copies[4:]:
        c.wait()
    out = pltpu.make_async_copy(w_ref, w_out, sems.at[7])
    out.start()
    copies[1].wait()
    score = jnp.sum(chosen * scores_ref[...], axis=1, keepdims=True)
    copies[2].wait()
    xd_ref[0:MOST] = dot(sel, tok_ref[...], NN).astype(BF)
    copies[3].wait()
    xd_ref[MOST:] = (score * dot(sel, grad_ref[...], NN)).astype(BF)
    out.wait()


def partial_body(blocks, *refs):
    w_own, w_oth, keep_ref = refs[blocks : blocks + 3]
    h = w_own.shape[0] // 3
    x = jnp.concatenate([r[0:MOST] for r in refs[:blocks]], axis=0)
    dz = jnp.concatenate([r[MOST:] for r in refs[:blocks]], axis=0)
    for at, a in ((slice(0, 2 * h), x), (slice(2 * h, 3 * h), dz)):
        keep_ref[at] = jnp.concatenate([dot(w[at], a, NT) for w in (w_own, w_oth)], axis=1)
    done = 0
    for send_ref in refs[blocks + 3 :]:
        send_ref[...] = keep_ref[done : done + send_ref.shape[0]].astype(BF)
        done += send_ref.shape[0]


def terms(keep, recv, dd_ref):
    h = keep.shape[0] // 3
    got = jnp.concatenate([r[...] for r in recv], axis=0).astype(F32)
    gate, upper, d_act = (keep[i * h : (i + 1) * h] + got[i * h : (i + 1) * h] for i in range(3))
    sigma = jax.nn.sigmoid(gate)
    gs = gate * sigma
    dd_ref[0:h] = (d_act * upper * sigma * (1.0 + gate * (1.0 - sigma))).astype(BF)
    dd_ref[h : 2 * h] = (d_act * gs).astype(BF)
    dd_ref[2 * h :] = (gs * upper).astype(BF)


def back_rows(dd, w_own, w_oth, dx_refs):
    at = slice(0, 2 * w_own.shape[0] // 3)
    m = dd.shape[1] // 2
    total = dot(dd[at], w_own[at], TN)[0:m] + dot(dd[at], w_oth[at], TN)[m:]
    for s, ref in enumerate(dx_refs):
        ref[...] = total[s * MOST : (s + 1) * MOST].astype(BF)


def first_body(recv, keep, *refs):
    w_own, w_oth, dd_ref, *dx_refs = refs[recv:]
    terms(keep, refs[:recv], dd_ref)
    back_rows(dd_ref, w_own, w_oth, dx_refs)


def second_body(blocks, keep, recv, w_own, w_oth, dd_a, *refs):
    early, refs = refs[: blocks // 2], refs[blocks // 2 :]
    dd_ref, rows_ref, *dx_refs = refs[blocks:]
    m = dd_a.shape[1]
    terms(keep, [recv], dd_ref.at[:, m:])
    back_rows(dd_ref.at[:, m:], w_own, w_oth, dx_refs[len(early) :])
    for a, ref in zip(early, dx_refs):
        ref[...] = a[...]
    dd_ref[:, 0:m] = dd_a[...]
    for s, block in enumerate(refs[:blocks]):
        rows_ref[s * MOST : (s + 1) * MOST] = block[0:MOST]
        rows_ref[(blocks + s) * MOST : (blocks + s + 1) * MOST] = block[MOST:]


def weights_body(coeff, rows_own, rows_oth, own, oth, gate_ref, up_ref, down_ref, token_ref):
    h = gate_ref.shape[0]
    m = rows_own.shape[0] // 4
    zero = jnp.zeros((m, rows_own.shape[1]), BF)
    for i, out in enumerate((gate_ref, up_ref, down_ref)):
        at = slice(i * h, (i + 1) * h)
        r = 0 if i < 2 else 2 * m
        mine = jnp.concatenate([rows_own[r : r + m], zero, rows_own[r + m : r + 2 * m], zero], axis=0)
        others = jnp.concatenate([zero, rows_oth[r : r + m], zero, rows_oth[r + m : r + 2 * m]], axis=0)
        one = dot(own[at], mine, NN)
        two = dot(oth[at], others, NN)
        out[...] = ((coeff * one).astype(BF).astype(F32) + (coeff * two).astype(BF).astype(F32)).astype(BF)
    token_ref[...] = jnp.zeros_like(token_ref)


def spread_body(sel_ref, *refs):
    total = refs[0][...].astype(F32)
    for r in refs[1:-1]:
        total += r[...].astype(F32)
    refs[-1][...] = dot(sel_ref[...], total.astype(BF), TN).astype(BF)


def swapped(tokens, grad_out, picks, scores, w_gate, w_up, w_down):
    n = lax.axis_size("seq")
    replicas = lax.axis_size("dp")
    tok_dev, half = tokens.shape[1:]
    cap = picks.shape[1]
    h = w_gate.shape[1]
    m = n // 2 * MOST
    coeff = float(replicas * cap) ** -0.5

    def index(d, k, t):
        return (k * 2 + d) * 2 + t

    def across(x, s):
        pairs = [(index(d, k, t), index(t, k ^ s, d)) for d in range(2) for k in range(n) for t in range(2)]
        return lax.ppermute(x, ("seq", "dp", "tensor"), pairs)

    def swap(x, axis):
        return lax.ppermute(x, axis, [(0, 1), (1, 0)])

    xd, sel, w_own = call(
        pack_body,
        [arr((2 * MOST, half)), arr((MOST, tok_dev)), arr((3 * h, half))],
        picks, scores, tokens[0], grad_out[0], w_gate.T, w_up.T, w_down,
        far=True, far_out=1, mib=60,
        scratch=[pltpu.VMEM((1, cap), jnp.int32), pltpu.VMEM((1, cap), F32), pltpu.VMEM((tok_dev, half), BF),
                 pltpu.VMEM((tok_dev, half), BF), pltpu.VMEM((3 * h, half), BF), pltpu.SemaphoreType.DMA((8,))],
    )
    blocks = {s: across(xd, s) for s in (2, 1, 0)}
    blocks[3] = lax.ppermute(blocks[2], "seq", [(k, k ^ 1) for k in range(n)])
    w_oth = swap(w_own, "tensor")
    flops = 2 * m * half * h

    def partial(group, parts, after=()):
        keep, *send = call(
            functools.partial(partial_body, len(group)),
            [arr((3 * h, 2 * m), F32)] + [arr((p * h, 2 * m)) for p in parts],
            *(blocks[s] for s in group), w_own, w_oth, flops=6 * flops, after=after,
        )
        return keep, [swap(b, "dp") for b in send]

    near, far = (0, 1), (2, 3)
    dx = [arr((MOST, half))] * (n // 2)
    keep_a, recv_a = partial(near, (3,))
    keep_b, recv_b = partial(far, (3,))
    dd_a, *dx_a = call(
        functools.partial(first_body, len(recv_a)), [arr((3 * h, 2 * m))] + dx,
        keep_a, *recv_a, w_own, w_oth, flops=8 * flops, after=(keep_b,),
    )
    own, rows_own, *dx = call(
        functools.partial(second_body, n), [arr((3 * h, 4 * m)), arr((2 * n * MOST, half))] + dx * 2,
        keep_b, *recv_b, w_own, w_oth, dd_a, *dx_a, *(blocks[s] for s in (*near, *far)), flops=8 * flops,
    )
    back = {s: across(b, s) for s, b in zip((*near, *far), dx)}
    rows_oth, oth = swap(rows_own, "tensor"), swap(own, "tensor")
    grads = call(
        functools.partial(weights_body, coeff), [arr((h, half))] * 3 + [arr((8, 128), F32)],
        rows_own, rows_oth, own, oth, flops=12 * flops,
    )
    (grad_local,) = call(spread_body, [arr((tok_dev, half))], sel, *(back[s] for s in (2, 3, 1, 0)), after=grads[3:])
    return grad_local[None], grads[0].T, grads[1].T, grads[2]


def gathered(tokens, grad_out, picks, scores, w_gate, w_up, w_down):
    tok_dev = tokens.shape[1]
    half = tokens.shape[2]
    seq_count = lax.axis_size("seq")
    ten_count = lax.axis_size("tensor")
    picks_row = picks[0]
    score_row = scores[0]
    cap = picks_row.shape[0]
    each = cap // (seq_count * ten_count)
    my_seq = lax.axis_index("seq")
    my_ten = lax.axis_index("tensor")
    my_replica = lax.axis_index("dp")
    share = w_gate.shape[0]
    full_gate, full_up, full_down = (
        lax.all_gather(w_gate, "dp", axis=0, tiled=True),
        lax.all_gather(w_up, "dp", axis=0, tiled=True),
        lax.all_gather(w_down, "dp", axis=1, tiled=True),
    )
    owner = picks_row // tok_dev
    mine = owner == my_seq
    place = jnp.clip(picks_row - my_seq * tok_dev, 0, tok_dev - 1)
    local_rows = tokens[0]
    local_grads = grad_out[0]
    zero_value = jnp.zeros((), jnp.bfloat16)
    shard_ids = jnp.arange(seq_count, dtype=jnp.int32)
    owner_table = (owner[:, None] == shard_ids[None, :]).astype(jnp.int32)
    earlier = jnp.cumsum(owner_table, axis=0) - owner_table
    slot_of = jnp.sum(earlier * owner_table, axis=1)
    slot_ids = jnp.arange(MOST, dtype=jnp.int32)
    match = (mine[None, :] & (slot_of[None, :] == slot_ids[:, None])).astype(jnp.int32)
    pick_ids = jnp.sum(match * jnp.arange(cap, dtype=jnp.int32)[None, :], axis=1)
    valid = jnp.sum(match, axis=1) > 0
    rows_at = jnp.clip(jnp.take(picks_row, pick_ids) - my_seq * tok_dev, 0, tok_dev - 1)
    pack_rows = jnp.where(valid[:, None], jnp.take(local_rows, rows_at, axis=0), zero_value)
    pack_grads = jnp.where(valid[:, None], jnp.take(local_grads, rows_at, axis=0), zero_value)
    all_rows, all_grads = (
        lax.all_gather(pack_rows, ("seq", "tensor"), axis=0, tiled=True),
        lax.all_gather(pack_grads, ("seq", "tensor"), axis=0, tiled=True),
    )

    def unpack(block):
        parts = [
            jnp.take(block, (owner * ten_count + part) * MOST + slot_of, axis=0)
            for part in range(ten_count)
        ]
        return jnp.concatenate(parts, axis=1)

    x_rows = unpack(all_rows)
    dy_rows = unpack(all_grads)
    dz = (score_row[:, None] * dy_rows.astype(jnp.float32)).astype(jnp.bfloat16)
    gate = jnp.dot(x_rows, full_gate, preferred_element_type=jnp.float32)
    upper = jnp.dot(x_rows, full_up, preferred_element_type=jnp.float32)
    sigma = jax.nn.sigmoid(gate)
    act = (gate * sigma * upper).astype(jnp.bfloat16)
    last_dims = (((1,), (1,)), ((), ()))
    first_dims = (((0,), (0,)), ((), ()))
    d_act = lax.dot_general(dz, full_down, last_dims, preferred_element_type=jnp.float32)
    d_gate = (d_act * upper * sigma * (1.0 + gate * (1.0 - sigma))).astype(jnp.bfloat16)
    d_up = (d_act * gate * sigma).astype(jnp.bfloat16)
    result = lax.dot_general(d_gate, full_gate, last_dims, preferred_element_type=jnp.float32)
    summed = lax.psum_scatter(
        result + lax.dot_general(d_up, full_up, last_dims, preferred_element_type=jnp.float32),
        ("seq", "tensor"),
        scatter_dimension=0,
        tiled=True,
    )
    coeff = float(lax.axis_size("dp") * cap) ** (-0.5)
    term_gate = (
        coeff * lax.dot_general(x_rows, d_gate, first_dims, preferred_element_type=jnp.float32)
    ).astype(jnp.bfloat16)
    term_up = (
        coeff * lax.dot_general(x_rows, d_up, first_dims, preferred_element_type=jnp.float32)
    ).astype(jnp.bfloat16)
    term_down = (
        coeff * lax.dot_general(act, dz, first_dims, preferred_element_type=jnp.float32)
    ).astype(jnp.bfloat16)
    sum_gate, sum_up, sum_down = (
        lax.psum(term_gate, "dp").astype(jnp.float32),
        lax.psum(term_up, "dp").astype(jnp.float32),
        lax.psum(term_down, "dp").astype(jnp.float32),
    )
    own_gate = lax.dynamic_slice_in_dim(sum_gate, my_replica * share, share, 0)
    own_up = lax.dynamic_slice_in_dim(sum_up, my_replica * share, share, 0)
    own_down = lax.dynamic_slice_in_dim(sum_down, my_replica * share, share, 1)
    my_block = my_seq * ten_count + my_ten
    block_owner = lax.dynamic_slice_in_dim(owner, my_block * each, each, 0)
    block_rows = summed.astype(jnp.bfloat16).reshape(each, ten_count, half).transpose(1, 0, 2)
    targets = block_owner[None, :] == jnp.arange(seq_count, dtype=jnp.int32)[:, None]
    outgoing = jnp.where(targets[:, None, :, None], block_rows[None], zero_value)
    incoming = lax.all_to_all(
        outgoing.reshape(seq_count * ten_count * each, half),
        ("seq", "tensor"),
        split_axis=0,
        concat_axis=0,
        tiled=True,
    )
    positions = jnp.arange(tok_dev, dtype=jnp.int32)
    selector = ((place[None, :] == positions[:, None]) & mine[None, :]).astype(jnp.bfloat16)
    grad_local = jnp.dot(selector, incoming, preferred_element_type=jnp.float32).astype(
        jnp.bfloat16
    )
    return (
        grad_local.reshape(1, tok_dev, half),
        own_gate.astype(jnp.bfloat16),
        own_up.astype(jnp.bfloat16),
        own_down.astype(jnp.bfloat16),
    )


def solution(mesh):
    in_specs = (
        P(("groups", "dp"), "seq", "tensor"),
        P(("groups", "dp"), "seq", "tensor"),
        P(("groups", "dp"), None),
        P(("groups", "dp"), None),
        P("dp", ("seq", "tensor")),
        P("dp", ("seq", "tensor")),
        P(("seq", "tensor"), "dp"),
    )
    out_specs = (
        P(("groups", "dp"), "seq", "tensor"),
        P(("groups", "dp"), ("seq", "tensor")),
        P(("groups", "dp"), ("seq", "tensor")),
        P(("groups", "seq", "tensor"), "dp"),
    )
    size = mesh.shape
    pairs = size["dp"] == size["tensor"] == 2 and size["seq"] in (2, 4, 8)
    local = swapped if pairs else gathered
    return jax.shard_map(local, mesh=mesh, in_specs=in_specs, out_specs=out_specs, check_vma=False)
```

```python
import functools

import jax
import jax.numpy as jnp
from jax import lax
from jax.experimental import pallas as pl
from jax.experimental.pallas import tpu as pltpu
from jax.sharding import PartitionSpec as P

MOST = 32
BF = jnp.bfloat16
F32 = jnp.float32
NN = (((1,), (0,)), ((), ()))
NT = (((1,), (1,)), ((), ()))
TN = (((0,), (0,)), ((), ()))


def dot(a, b, dims):
    return lax.dot_general(a, b, dims, preferred_element_type=F32)


def call(body, outs, *args, flops=0, after=(), far=False, scratch=(), mib=24, far_out=0):
    size = sum(a.size * a.dtype.itemsize for a in args) + sum(o.size * o.dtype.itemsize for o in outs)
    count = len(args)

    def run(*refs):
        body(*refs[:count], *refs[count + len(after) :])

    return pl.pallas_call(
        run,
        out_shape=outs,
        in_specs=[pl.BlockSpec(memory_space=pltpu.HBM if far else pltpu.VMEM)] * len(args)
        + [pl.BlockSpec(memory_space=pl.ANY)] * len(after),
        out_specs=[pl.BlockSpec(memory_space=pltpu.VMEM)] * (len(outs) - far_out) + [pl.BlockSpec(memory_space=pltpu.HBM)] * far_out,
        scratch_shapes=list(scratch),
        cost_estimate=pl.CostEstimate(flops=flops, bytes_accessed=size, transcendentals=0),
        compiler_params=pltpu.CompilerParams(vmem_limit_bytes=int(mib * 1024 * 1024)),
    )(*args, *after)


def arr(shape, dtype=BF):
    return jax.ShapeDtypeStruct(shape, dtype)


def pack_body(picks_in, scores_in, tok_in, grad_in, gate_in, up_in, down_in, xd_ref, sel_ref, w_out, picks_ref, scores_ref, tok_ref, grad_ref, sems):
    pairs = [(picks_in, picks_ref), (scores_in, scores_ref), (tok_in, tok_ref), (grad_in, grad_ref)]
    h = gate_in.shape[0]
    pairs += [(w, w_out.at[i * h : (i + 1) * h]) for i, w in enumerate((gate_in, up_in, down_in))]
    copies = [pltpu.make_async_copy(a, b, sems.at[i]) for i, (a, b) in enumerate(pairs)]
    for c in copies:
        c.start()
    tok_dev = tok_ref.shape[0]
    cap = picks_ref.shape[1]
    base = lax.axis_index("seq") * tok_dev
    before = (
        lax.broadcasted_iota(jnp.int32, (tok_dev, tok_dev), 0) < lax.broadcasted_iota(jnp.int32, (tok_dev, tok_dev), 1)
    ).astype(F32).astype(BF)
    slots = lax.broadcasted_iota(jnp.int32, (MOST, tok_dev), 0).astype(F32)
    copies[0].wait()
    where = picks_ref[...] - base
    hit = (lax.broadcasted_iota(jnp.int32, (tok_dev, cap), 0) == where).astype(F32).astype(BF)
    picked = dot(jnp.ones((8, cap), BF), hit, NT)
    rank = dot(picked.astype(BF), before, NN)[0:1]
    sel = jnp.where((rank == slots) & (picked[0:1] > 0.5), 1.0, 0.0).astype(BF)
    sel_ref[...] = sel
    chosen = dot(sel, hit, NN)
    copies[1].wait()
    score = jnp.sum(chosen * scores_ref[...], axis=1, keepdims=True)
    copies[2].wait()
    xd_ref[0:MOST] = dot(sel, tok_ref[...], NN).astype(BF)
    copies[3].wait()
    xd_ref[MOST:] = (score * dot(sel, grad_ref[...], NN)).astype(BF)
    for c in copies[4:]:
        c.wait()


def partial_body(blocks, *refs):
    w_own, w_oth, keep_ref = refs[blocks : blocks + 3]
    h = w_own.shape[0] // 3
    x = jnp.concatenate([r[0:MOST] for r in refs[:blocks]], axis=0)
    dz = jnp.concatenate([r[MOST:] for r in refs[:blocks]], axis=0)
    for at, a in ((slice(0, 2 * h), x), (slice(2 * h, 3 * h), dz)):
        keep_ref[at] = jnp.concatenate([dot(w[at], a, NT) for w in (w_own, w_oth)], axis=1)
    done = 0
    for send_ref in refs[blocks + 3 :]:
        send_ref[...] = keep_ref[done : done + send_ref.shape[0]].astype(BF)
        done += send_ref.shape[0]


def terms(keep, recv, dd_ref):
    h = keep.shape[0] // 3
    got = jnp.concatenate([r[...] for r in recv], axis=0).astype(F32)
    gate, upper, d_act = (keep[i * h : (i + 1) * h] + got[i * h : (i + 1) * h] for i in range(3))
    sigma = jax.nn.sigmoid(gate)
    gs = gate * sigma
    dd_ref[0:h] = (d_act * upper * sigma * (1.0 + gate * (1.0 - sigma))).astype(BF)
    dd_ref[h : 2 * h] = (d_act * gs).astype(BF)
    dd_ref[2 * h :] = (gs * upper).astype(BF)


def back_rows(dd, w_own, w_oth, dx_refs):
    at = slice(0, 2 * w_own.shape[0] // 3)
    m = dd.shape[1] // 2
    total = dot(dd[at], w_own[at], TN)[0:m] + dot(dd[at], w_oth[at], TN)[m:]
    for s, ref in enumerate(dx_refs):
        ref[...] = total[s * MOST : (s + 1) * MOST].astype(BF)


def first_body(recv, keep, *refs):
    w_own, w_oth, dd_ref, *dx_refs = refs[recv:]
    terms(keep, refs[:recv], dd_ref)
    back_rows(dd_ref, w_own, w_oth, dx_refs)


def second_body(blocks, keep, recv, w_own, w_oth, dd_a, *refs):
    early, refs = refs[: blocks // 2], refs[blocks // 2 :]
    dd_ref, rows_ref, *dx_refs = refs[blocks:]
    m = dd_a.shape[1]
    terms(keep, [recv], dd_ref.at[:, m:])
    back_rows(dd_ref.at[:, m:], w_own, w_oth, dx_refs[len(early) :])
    for a, ref in zip(early, dx_refs):
        ref[...] = a[...]
    dd_ref[:, 0:m] = dd_a[...]
    for s, block in enumerate(refs[:blocks]):
        rows_ref[s * MOST : (s + 1) * MOST] = block[0:MOST]
        rows_ref[(blocks + s) * MOST : (blocks + s + 1) * MOST] = block[MOST:]


def weights_body(coeff, rows_own, rows_oth, own, oth, gate_ref, up_ref, down_ref, token_ref):
    h = gate_ref.shape[0]
    m = rows_own.shape[0] // 4
    zero = jnp.zeros((m, rows_own.shape[1]), BF)
    for i, out in enumerate((gate_ref, up_ref, down_ref)):
        at = slice(i * h, (i + 1) * h)
        r = 0 if i < 2 else 2 * m
        mine = jnp.concatenate([rows_own[r : r + m], zero, rows_own[r + m : r + 2 * m], zero], axis=0)
        others = jnp.concatenate([zero, rows_oth[r : r + m], zero, rows_oth[r + m : r + 2 * m]], axis=0)
        one = dot(own[at], mine, NN)
        two = dot(oth[at], others, NN)
        out[...] = ((coeff * one).astype(BF).astype(F32) + (coeff * two).astype(BF).astype(F32)).astype(BF)
    token_ref[...] = jnp.zeros_like(token_ref)


def spread_body(sel_ref, *refs):
    total = refs[0][...].astype(F32)
    for r in refs[1:-1]:
        total += r[...].astype(F32)
    refs[-1][...] = dot(sel_ref[...], total.astype(BF), TN).astype(BF)


def swapped(tokens, grad_out, picks, scores, w_gate, w_up, w_down):
    n = lax.axis_size("seq")
    replicas = lax.axis_size("dp")
    tok_dev, half = tokens.shape[1:]
    cap = picks.shape[1]
    h = w_gate.shape[1]
    m = n // 2 * MOST
    coeff = float(replicas * cap) ** -0.5

    def index(d, k, t):
        return (k * 2 + d) * 2 + t

    def across(x, s):
        pairs = [(index(d, k, t), index(t, k ^ s, d)) for d in range(2) for k in range(n) for t in range(2)]
        return lax.ppermute(x, ("seq", "dp", "tensor"), pairs)

    def swap(x, axis):
        return lax.ppermute(x, axis, [(0, 1), (1, 0)])

    xd, sel, w_own = call(
        pack_body,
        [arr((2 * MOST, half)), arr((MOST, tok_dev)), arr((3 * h, half))],
        *(pltpu.with_memory_space_constraint(a, pltpu.HBM) for a in (picks, scores, tokens[0], grad_out[0], w_gate.T, w_up.T, w_down)),
        far=True, mib=24,
        scratch=[pltpu.VMEM((1, cap), jnp.int32), pltpu.VMEM((1, cap), F32), pltpu.VMEM((tok_dev, half), BF),
                 pltpu.VMEM((tok_dev, half), BF), pltpu.SemaphoreType.DMA((7,))],
    )
    blocks = {s: across(xd, s) for s in (2, 1, 0)}
    blocks[3] = lax.ppermute(blocks[2], "seq", [(k, k ^ 1) for k in range(n)])
    w_oth = swap(w_own, "tensor")
    flops = 2 * m * half * h

    def partial(group, parts, after=()):
        keep, *send = call(
            functools.partial(partial_body, len(group)),
            [arr((3 * h, 2 * m), F32)] + [arr((p * h, 2 * m)) for p in parts],
            *(blocks[s] for s in group), w_own, w_oth, flops=6 * flops, after=after,
        )
        return keep, [swap(b, "dp") for b in send]

    near, far = (0, 1), (2, 3)
    dx = [arr((MOST, half))] * (n // 2)
    keep_a, recv_a = partial(near, (3,))
    keep_b, recv_b = partial(far, (3,))
    dd_a, *dx_a = call(
        functools.partial(first_body, len(recv_a)), [arr((3 * h, 2 * m))] + dx,
        keep_a, *recv_a, w_own, w_oth, flops=8 * flops, after=(keep_b,),
    )
    own, rows_own, *dx = call(
        functools.partial(second_body, n), [arr((3 * h, 4 * m)), arr((2 * n * MOST, half))] + dx * 2,
        keep_b, *recv_b, w_own, w_oth, dd_a, *dx_a, *(blocks[s] for s in (*near, *far)), flops=8 * flops,
    )
    back = {s: across(b, s) for s, b in zip((*near, *far), dx)}
    rows_oth, oth = swap(rows_own, "tensor"), swap(own, "tensor")
    grads = call(
        functools.partial(weights_body, coeff), [arr((h, half))] * 3 + [arr((8, 128), F32)],
        rows_own, rows_oth, own, oth, flops=12 * flops,
    )
    (grad_local,) = call(spread_body, [arr((tok_dev, half))], sel, *(back[s] for s in (2, 3, 1, 0)), after=grads[3:])
    return grad_local[None], grads[0].T, grads[1].T, grads[2]


def gathered(tokens, grad_out, picks, scores, w_gate, w_up, w_down):
    tok_dev = tokens.shape[1]
    half = tokens.shape[2]
    seq_count = lax.axis_size("seq")
    ten_count = lax.axis_size("tensor")
    picks_row = picks[0]
    score_row = scores[0]
    cap = picks_row.shape[0]
    each = cap // (seq_count * ten_count)
    my_seq = lax.axis_index("seq")
    my_ten = lax.axis_index("tensor")
    my_replica = lax.axis_index("dp")
    share = w_gate.shape[0]
    full_gate, full_up, full_down = (
        lax.all_gather(w_gate, "dp", axis=0, tiled=True),
        lax.all_gather(w_up, "dp", axis=0, tiled=True),
        lax.all_gather(w_down, "dp", axis=1, tiled=True),
    )
    owner = picks_row // tok_dev
    mine = owner == my_seq
    place = jnp.clip(picks_row - my_seq * tok_dev, 0, tok_dev - 1)
    local_rows = tokens[0]
    local_grads = grad_out[0]
    zero_value = jnp.zeros((), jnp.bfloat16)
    shard_ids = jnp.arange(seq_count, dtype=jnp.int32)
    owner_table = (owner[:, None] == shard_ids[None, :]).astype(jnp.int32)
    earlier = jnp.cumsum(owner_table, axis=0) - owner_table
    slot_of = jnp.sum(earlier * owner_table, axis=1)
    slot_ids = jnp.arange(MOST, dtype=jnp.int32)
    match = (mine[None, :] & (slot_of[None, :] == slot_ids[:, None])).astype(jnp.int32)
    pick_ids = jnp.sum(match * jnp.arange(cap, dtype=jnp.int32)[None, :], axis=1)
    valid = jnp.sum(match, axis=1) > 0
    rows_at = jnp.clip(jnp.take(picks_row, pick_ids) - my_seq * tok_dev, 0, tok_dev - 1)
    pack_rows = jnp.where(valid[:, None], jnp.take(local_rows, rows_at, axis=0), zero_value)
    pack_grads = jnp.where(valid[:, None], jnp.take(local_grads, rows_at, axis=0), zero_value)
    all_rows, all_grads = (
        lax.all_gather(pack_rows, ("seq", "tensor"), axis=0, tiled=True),
        lax.all_gather(pack_grads, ("seq", "tensor"), axis=0, tiled=True),
    )

    def unpack(block):
        parts = [
            jnp.take(block, (owner * ten_count + part) * MOST + slot_of, axis=0)
            for part in range(ten_count)
        ]
        return jnp.concatenate(parts, axis=1)

    x_rows = unpack(all_rows)
    dy_rows = unpack(all_grads)
    dz = (score_row[:, None] * dy_rows.astype(jnp.float32)).astype(jnp.bfloat16)
    gate = jnp.dot(x_rows, full_gate, preferred_element_type=jnp.float32)
    upper = jnp.dot(x_rows, full_up, preferred_element_type=jnp.float32)
    sigma = jax.nn.sigmoid(gate)
    act = (gate * sigma * upper).astype(jnp.bfloat16)
    last_dims = (((1,), (1,)), ((), ()))
    first_dims = (((0,), (0,)), ((), ()))
    d_act = lax.dot_general(dz, full_down, last_dims, preferred_element_type=jnp.float32)
    d_gate = (d_act * upper * sigma * (1.0 + gate * (1.0 - sigma))).astype(jnp.bfloat16)
    d_up = (d_act * gate * sigma).astype(jnp.bfloat16)
    result = lax.dot_general(d_gate, full_gate, last_dims, preferred_element_type=jnp.float32)
    summed = lax.psum_scatter(
        result + lax.dot_general(d_up, full_up, last_dims, preferred_element_type=jnp.float32),
        ("seq", "tensor"),
        scatter_dimension=0,
        tiled=True,
    )
    coeff = float(lax.axis_size("dp") * cap) ** (-0.5)
    term_gate = (
        coeff * lax.dot_general(x_rows, d_gate, first_dims, preferred_element_type=jnp.float32)
    ).astype(jnp.bfloat16)
    term_up = (
        coeff * lax.dot_general(x_rows, d_up, first_dims, preferred_element_type=jnp.float32)
    ).astype(jnp.bfloat16)
    term_down = (
        coeff * lax.dot_general(act, dz, first_dims, preferred_element_type=jnp.float32)
    ).astype(jnp.bfloat16)
    sum_gate, sum_up, sum_down = (
        lax.psum(term_gate, "dp").astype(jnp.float32),
        lax.psum(term_up, "dp").astype(jnp.float32),
        lax.psum(term_down, "dp").astype(jnp.float32),
    )
    own_gate = lax.dynamic_slice_in_dim(sum_gate, my_replica * share, share, 0)
    own_up = lax.dynamic_slice_in_dim(sum_up, my_replica * share, share, 0)
    own_down = lax.dynamic_slice_in_dim(sum_down, my_replica * share, share, 1)
    my_block = my_seq * ten_count + my_ten
    block_owner = lax.dynamic_slice_in_dim(owner, my_block * each, each, 0)
    block_rows = summed.astype(jnp.bfloat16).reshape(each, ten_count, half).transpose(1, 0, 2)
    targets = block_owner[None, :] == jnp.arange(seq_count, dtype=jnp.int32)[:, None]
    outgoing = jnp.where(targets[:, None, :, None], block_rows[None], zero_value)
    incoming = lax.all_to_all(
        outgoing.reshape(seq_count * ten_count * each, half),
        ("seq", "tensor"),
        split_axis=0,
        concat_axis=0,
        tiled=True,
    )
    positions = jnp.arange(tok_dev, dtype=jnp.int32)
    selector = ((place[None, :] == positions[:, None]) & mine[None, :]).astype(jnp.bfloat16)
    grad_local = jnp.dot(selector, incoming, preferred_element_type=jnp.float32).astype(
        jnp.bfloat16
    )
    return (
        grad_local.reshape(1, tok_dev, half),
        own_gate.astype(jnp.bfloat16),
        own_up.astype(jnp.bfloat16),
        own_down.astype(jnp.bfloat16),
    )


def solution(mesh):
    in_specs = (
        P(("groups", "dp"), "seq", "tensor"),
        P(("groups", "dp"), "seq", "tensor"),
        P(("groups", "dp"), None),
        P(("groups", "dp"), None),
        P("dp", ("seq", "tensor")),
        P("dp", ("seq", "tensor")),
        P(("seq", "tensor"), "dp"),
    )
    out_specs = (
        P(("groups", "dp"), "seq", "tensor"),
        P(("groups", "dp"), ("seq", "tensor")),
        P(("groups", "dp"), ("seq", "tensor")),
        P(("groups", "seq", "tensor"), "dp"),
    )
    size = mesh.shape
    pairs = size["dp"] == size["tensor"] == 2 and size["seq"] in (2, 4, 8)
    local = swapped if pairs else gathered
    return jax.shard_map(local, mesh=mesh, in_specs=in_specs, out_specs=out_specs, check_vma=False)
```

```python
import functools

import jax
import jax.numpy as jnp
from jax import lax
from jax.experimental import pallas as pl
from jax.experimental.pallas import tpu as pltpu
from jax.sharding import PartitionSpec as P

MOST = 32
BF = jnp.bfloat16
F32 = jnp.float32
NN = (((1,), (0,)), ((), ()))
NT = (((1,), (1,)), ((), ()))
TN = (((0,), (0,)), ((), ()))


def dot(a, b, dims):
    return lax.dot_general(a, b, dims, preferred_element_type=F32)


def call(body, outs, *args, flops=0, after=(), far=False, scratch=(), mib=24, far_out=0):
    size = sum(a.size * a.dtype.itemsize for a in args) + sum(o.size * o.dtype.itemsize for o in outs)
    count = len(args)

    def run(*refs):
        body(*refs[:count], *refs[count + len(after) :])

    return pl.pallas_call(
        run,
        out_shape=outs,
        in_specs=[pl.BlockSpec(memory_space=pltpu.HBM if far else pltpu.VMEM)] * len(args)
        + [pl.BlockSpec(memory_space=pl.ANY)] * len(after),
        out_specs=[pl.BlockSpec(memory_space=pltpu.VMEM)] * (len(outs) - far_out) + [pl.BlockSpec(memory_space=pltpu.HBM)] * far_out,
        scratch_shapes=list(scratch),
        cost_estimate=pl.CostEstimate(flops=flops, bytes_accessed=size, transcendentals=0),
        compiler_params=pltpu.CompilerParams(vmem_limit_bytes=int(mib * 1024 * 1024)),
    )(*args, *after)


def arr(shape, dtype=BF):
    return jax.ShapeDtypeStruct(shape, dtype)


def pack_body(picks_in, scores_in, tok_in, grad_in, gate_in, up_in, down_in, xd_ref, sel_ref, w_out, picks_ref, scores_ref, tok_ref, grad_ref, sems):
    pairs = [(picks_in, picks_ref), (scores_in, scores_ref), (tok_in, tok_ref), (grad_in, grad_ref)]
    h = gate_in.shape[0]
    pairs += [(w, w_out.at[i * h : (i + 1) * h]) for i, w in enumerate((gate_in, up_in, down_in))]
    copies = [pltpu.make_async_copy(a, b, sems.at[i]) for i, (a, b) in enumerate(pairs)]
    for c in copies:
        c.start()
    tok_dev = tok_ref.shape[0]
    cap = picks_ref.shape[1]
    base = lax.axis_index("seq") * tok_dev
    before = (
        lax.broadcasted_iota(jnp.int32, (tok_dev, tok_dev), 0) < lax.broadcasted_iota(jnp.int32, (tok_dev, tok_dev), 1)
    ).astype(F32).astype(BF)
    slots = lax.broadcasted_iota(jnp.int32, (MOST, tok_dev), 0).astype(F32)
    copies[0].wait()
    where = picks_ref[...] - base
    hit = (lax.broadcasted_iota(jnp.int32, (tok_dev, cap), 0) == where).astype(F32).astype(BF)
    picked = dot(jnp.ones((8, cap), BF), hit, NT)
    rank = dot(picked.astype(BF), before, NN)[0:1]
    sel = jnp.where((rank == slots) & (picked[0:1] > 0.5), 1.0, 0.0).astype(BF)
    sel_ref[...] = sel
    chosen = dot(sel, hit, NN)
    copies[1].wait()
    score = jnp.sum(chosen * scores_ref[...], axis=1, keepdims=True)
    copies[2].wait()
    xd_ref[0:MOST] = dot(sel, tok_ref[...], NN).astype(BF)
    copies[3].wait()
    xd_ref[MOST:] = (score * dot(sel, grad_ref[...], NN)).astype(BF)
    for c in copies[4:]:
        c.wait()


def partial_body(blocks, *refs):
    w_own, w_oth, keep_ref = refs[blocks : blocks + 3]
    h = w_own.shape[0] // 3
    x = jnp.concatenate([r[0:MOST] for r in refs[:blocks]], axis=0)
    dz = jnp.concatenate([r[MOST:] for r in refs[:blocks]], axis=0)
    for at, a in ((slice(0, 2 * h), x), (slice(2 * h, 3 * h), dz)):
        keep_ref[at] = jnp.concatenate([dot(w[at], a, NT) for w in (w_own, w_oth)], axis=1)
    done = 0
    for send_ref in refs[blocks + 3 :]:
        send_ref[...] = keep_ref[done : done + send_ref.shape[0]].astype(BF)
        done += send_ref.shape[0]


def terms(keep, recv, dd_ref):
    h = keep.shape[0] // 3
    got = jnp.concatenate([r[...] for r in recv], axis=0).astype(F32)
    gate, upper, d_act = (keep[i * h : (i + 1) * h] + got[i * h : (i + 1) * h] for i in range(3))
    sigma = jax.nn.sigmoid(gate)
    gs = gate * sigma
    dd_ref[0:h] = (d_act * upper * sigma * (1.0 + gate * (1.0 - sigma))).astype(BF)
    dd_ref[h : 2 * h] = (d_act * gs).astype(BF)
    dd_ref[2 * h :] = (gs * upper).astype(BF)


def back_rows(dd, w_own, w_oth, dx_refs):
    at = slice(0, 2 * w_own.shape[0] // 3)
    m = dd.shape[1] // 2
    total = dot(dd[at], w_own[at], TN)[0:m] + dot(dd[at], w_oth[at], TN)[m:]
    for s, ref in enumerate(dx_refs):
        ref[...] = total[s * MOST : (s + 1) * MOST].astype(BF)


def first_body(recv, keep, *refs):
    w_own, w_oth, dd_ref, *dx_refs = refs[recv:]
    terms(keep, refs[:recv], dd_ref)
    back_rows(dd_ref, w_own, w_oth, dx_refs)


def second_body(blocks, keep, recv, w_own, w_oth, dd_a, *refs):
    early, refs = refs[: blocks // 2], refs[blocks // 2 :]
    dd_ref, rows_ref, *dx_refs = refs[blocks:]
    m = dd_a.shape[1]
    terms(keep, [recv], dd_ref.at[:, m:])
    back_rows(dd_ref.at[:, m:], w_own, w_oth, dx_refs[len(early) :])
    for a, ref in zip(early, dx_refs):
        ref[...] = a[...]
    dd_ref[:, 0:m] = dd_a[...]
    for s, block in enumerate(refs[:blocks]):
        rows_ref[s * MOST : (s + 1) * MOST] = block[0:MOST]
        rows_ref[(blocks + s) * MOST : (blocks + s + 1) * MOST] = block[MOST:]


def weights_body(coeff, rows_own, rows_oth, own, oth, gate_ref, up_ref, down_ref, token_ref):
    h = gate_ref.shape[0]
    m = rows_own.shape[0] // 4
    zero = jnp.zeros((m, rows_own.shape[1]), BF)
    for i, out in enumerate((gate_ref, up_ref, down_ref)):
        at = slice(i * h, (i + 1) * h)
        r = 0 if i < 2 else 2 * m
        mine = jnp.concatenate([rows_own[r : r + m], zero, rows_own[r + m : r + 2 * m], zero], axis=0)
        others = jnp.concatenate([zero, rows_oth[r : r + m], zero, rows_oth[r + m : r + 2 * m]], axis=0)
        one = dot(own[at], mine, NN)
        two = dot(oth[at], others, NN)
        out[...] = ((coeff * one).astype(BF).astype(F32) + (coeff * two).astype(BF).astype(F32)).astype(BF)
    token_ref[...] = jnp.zeros_like(token_ref)


def spread_body(sel_ref, *refs):
    total = refs[0][...].astype(F32)
    for r in refs[1:-1]:
        total += r[...].astype(F32)
    refs[-1][...] = dot(sel_ref[...], total.astype(BF), TN).astype(BF)


def swapped(tokens, grad_out, picks, scores, w_gate, w_up, w_down):
    n = lax.axis_size("seq")
    replicas = lax.axis_size("dp")
    tok_dev, half = tokens.shape[1:]
    cap = picks.shape[1]
    h = w_gate.shape[1]
    m = n // 2 * MOST
    coeff = float(replicas * cap) ** -0.5

    def index(d, k, t):
        return (k * 2 + d) * 2 + t

    def across(x, s):
        pairs = [(index(d, k, t), index(t, k ^ s, d)) for d in range(2) for k in range(n) for t in range(2)]
        return lax.ppermute(x, ("seq", "dp", "tensor"), pairs)

    def swap(x, axis):
        return lax.ppermute(x, axis, [(0, 1), (1, 0)])

    xd, sel, w_own = call(
        pack_body,
        [arr((2 * MOST, half)), arr((MOST, tok_dev)), arr((3 * h, half))],
        *(pltpu.with_memory_space_constraint(a, pltpu.HBM) for a in (picks, scores, tokens[0], grad_out[0], w_gate.T, w_up.T, w_down)),
        far=True, mib=24,
        scratch=[pltpu.VMEM((1, cap), jnp.int32), pltpu.VMEM((1, cap), F32), pltpu.VMEM((tok_dev, half), BF),
                 pltpu.VMEM((tok_dev, half), BF), pltpu.SemaphoreType.DMA((7,))],
    )
    blocks = {s: across(xd, s) for s in (2, 1, 0)}
    blocks[3] = lax.ppermute(blocks[2], "seq", [(k, k ^ 1) for k in range(n)])
    w_oth = swap(w_own, "tensor")
    flops = 2 * m * half * h

    def partial(group, parts, after=()):
        keep, *send = call(
            functools.partial(partial_body, len(group)),
            [arr((3 * h, 2 * m), F32)] + [arr((p * h, 2 * m)) for p in parts],
            *(blocks[s] for s in group), w_own, w_oth, flops=6 * flops, after=after,
        )
        return keep, [swap(b, "dp") for b in send]

    near, far = (1, 2), (0, 3)
    dx = [arr((MOST, half))] * (n // 2)
    keep_a, recv_a = partial(near, (3,))
    keep_b, recv_b = partial(far, (3,))
    dd_a, *dx_a = call(
        functools.partial(first_body, len(recv_a)), [arr((3 * h, 2 * m))] + dx,
        keep_a, *recv_a, w_own, w_oth, flops=8 * flops, after=(keep_b,),
    )
    own, rows_own, *dx = call(
        functools.partial(second_body, n), [arr((3 * h, 4 * m)), arr((2 * n * MOST, half))] + dx * 2,
        keep_b, *recv_b, w_own, w_oth, dd_a, *dx_a, *(blocks[s] for s in (*near, *far)), flops=8 * flops,
    )
    back = {s: across(b, s) for s, b in zip((*near, *far), dx)}
    rows_oth, oth = swap(rows_own, "tensor"), swap(own, "tensor")
    grads = call(
        functools.partial(weights_body, coeff), [arr((h, half))] * 3 + [arr((8, 128), F32)],
        rows_own, rows_oth, own, oth, flops=12 * flops,
    )
    (grad_local,) = call(spread_body, [arr((tok_dev, half))], sel, *(back[s] for s in (2, 3, 1, 0)), after=grads[3:])
    return grad_local[None], grads[0].T, grads[1].T, grads[2]


def gathered(tokens, grad_out, picks, scores, w_gate, w_up, w_down):
    tok_dev = tokens.shape[1]
    half = tokens.shape[2]
    seq_count = lax.axis_size("seq")
    ten_count = lax.axis_size("tensor")
    picks_row = picks[0]
    score_row = scores[0]
    cap = picks_row.shape[0]
    each = cap // (seq_count * ten_count)
    my_seq = lax.axis_index("seq")
    my_ten = lax.axis_index("tensor")
    my_replica = lax.axis_index("dp")
    share = w_gate.shape[0]
    full_gate, full_up, full_down = (
        lax.all_gather(w_gate, "dp", axis=0, tiled=True),
        lax.all_gather(w_up, "dp", axis=0, tiled=True),
        lax.all_gather(w_down, "dp", axis=1, tiled=True),
    )
    owner = picks_row // tok_dev
    mine = owner == my_seq
    place = jnp.clip(picks_row - my_seq * tok_dev, 0, tok_dev - 1)
    local_rows = tokens[0]
    local_grads = grad_out[0]
    zero_value = jnp.zeros((), jnp.bfloat16)
    shard_ids = jnp.arange(seq_count, dtype=jnp.int32)
    owner_table = (owner[:, None] == shard_ids[None, :]).astype(jnp.int32)
    earlier = jnp.cumsum(owner_table, axis=0) - owner_table
    slot_of = jnp.sum(earlier * owner_table, axis=1)
    slot_ids = jnp.arange(MOST, dtype=jnp.int32)
    match = (mine[None, :] & (slot_of[None, :] == slot_ids[:, None])).astype(jnp.int32)
    pick_ids = jnp.sum(match * jnp.arange(cap, dtype=jnp.int32)[None, :], axis=1)
    valid = jnp.sum(match, axis=1) > 0
    rows_at = jnp.clip(jnp.take(picks_row, pick_ids) - my_seq * tok_dev, 0, tok_dev - 1)
    pack_rows = jnp.where(valid[:, None], jnp.take(local_rows, rows_at, axis=0), zero_value)
    pack_grads = jnp.where(valid[:, None], jnp.take(local_grads, rows_at, axis=0), zero_value)
    all_rows, all_grads = (
        lax.all_gather(pack_rows, ("seq", "tensor"), axis=0, tiled=True),
        lax.all_gather(pack_grads, ("seq", "tensor"), axis=0, tiled=True),
    )

    def unpack(block):
        parts = [
            jnp.take(block, (owner * ten_count + part) * MOST + slot_of, axis=0)
            for part in range(ten_count)
        ]
        return jnp.concatenate(parts, axis=1)

    x_rows = unpack(all_rows)
    dy_rows = unpack(all_grads)
    dz = (score_row[:, None] * dy_rows.astype(jnp.float32)).astype(jnp.bfloat16)
    gate = jnp.dot(x_rows, full_gate, preferred_element_type=jnp.float32)
    upper = jnp.dot(x_rows, full_up, preferred_element_type=jnp.float32)
    sigma = jax.nn.sigmoid(gate)
    act = (gate * sigma * upper).astype(jnp.bfloat16)
    last_dims = (((1,), (1,)), ((), ()))
    first_dims = (((0,), (0,)), ((), ()))
    d_act = lax.dot_general(dz, full_down, last_dims, preferred_element_type=jnp.float32)
    d_gate = (d_act * upper * sigma * (1.0 + gate * (1.0 - sigma))).astype(jnp.bfloat16)
    d_up = (d_act * gate * sigma).astype(jnp.bfloat16)
    result = lax.dot_general(d_gate, full_gate, last_dims, preferred_element_type=jnp.float32)
    summed = lax.psum_scatter(
        result + lax.dot_general(d_up, full_up, last_dims, preferred_element_type=jnp.float32),
        ("seq", "tensor"),
        scatter_dimension=0,
        tiled=True,
    )
    coeff = float(lax.axis_size("dp") * cap) ** (-0.5)
    term_gate = (
        coeff * lax.dot_general(x_rows, d_gate, first_dims, preferred_element_type=jnp.float32)
    ).astype(jnp.bfloat16)
    term_up = (
        coeff * lax.dot_general(x_rows, d_up, first_dims, preferred_element_type=jnp.float32)
    ).astype(jnp.bfloat16)
    term_down = (
        coeff * lax.dot_general(act, dz, first_dims, preferred_element_type=jnp.float32)
    ).astype(jnp.bfloat16)
    sum_gate, sum_up, sum_down = (
        lax.psum(term_gate, "dp").astype(jnp.float32),
        lax.psum(term_up, "dp").astype(jnp.float32),
        lax.psum(term_down, "dp").astype(jnp.float32),
    )
    own_gate = lax.dynamic_slice_in_dim(sum_gate, my_replica * share, share, 0)
    own_up = lax.dynamic_slice_in_dim(sum_up, my_replica * share, share, 0)
    own_down = lax.dynamic_slice_in_dim(sum_down, my_replica * share, share, 1)
    my_block = my_seq * ten_count + my_ten
    block_owner = lax.dynamic_slice_in_dim(owner, my_block * each, each, 0)
    block_rows = summed.astype(jnp.bfloat16).reshape(each, ten_count, half).transpose(1, 0, 2)
    targets = block_owner[None, :] == jnp.arange(seq_count, dtype=jnp.int32)[:, None]
    outgoing = jnp.where(targets[:, None, :, None], block_rows[None], zero_value)
    incoming = lax.all_to_all(
        outgoing.reshape(seq_count * ten_count * each, half),
        ("seq", "tensor"),
        split_axis=0,
        concat_axis=0,
        tiled=True,
    )
    positions = jnp.arange(tok_dev, dtype=jnp.int32)
    selector = ((place[None, :] == positions[:, None]) & mine[None, :]).astype(jnp.bfloat16)
    grad_local = jnp.dot(selector, incoming, preferred_element_type=jnp.float32).astype(
        jnp.bfloat16
    )
    return (
        grad_local.reshape(1, tok_dev, half),
        own_gate.astype(jnp.bfloat16),
        own_up.astype(jnp.bfloat16),
        own_down.astype(jnp.bfloat16),
    )


def solution(mesh):
    in_specs = (
        P(("groups", "dp"), "seq", "tensor"),
        P(("groups", "dp"), "seq", "tensor"),
        P(("groups", "dp"), None),
        P(("groups", "dp"), None),
        P("dp", ("seq", "tensor")),
        P("dp", ("seq", "tensor")),
        P(("seq", "tensor"), "dp"),
    )
    out_specs = (
        P(("groups", "dp"), "seq", "tensor"),
        P(("groups", "dp"), ("seq", "tensor")),
        P(("groups", "dp"), ("seq", "tensor")),
        P(("groups", "seq", "tensor"), "dp"),
    )
    size = mesh.shape
    pairs = size["dp"] == size["tensor"] == 2 and size["seq"] == 4
    local = swapped if pairs else gathered
    return jax.shard_map(local, mesh=mesh, in_specs=in_specs, out_specs=out_specs, check_vma=False)
```

```python
import functools

import jax
import jax.numpy as jnp
from jax import lax
from jax.experimental import pallas as pl
from jax.experimental.pallas import tpu as pltpu
from jax.sharding import PartitionSpec as P

MOST = 32
BF = jnp.bfloat16
F32 = jnp.float32
NN = (((1,), (0,)), ((), ()))
NT = (((1,), (1,)), ((), ()))
TN = (((0,), (0,)), ((), ()))


def dot(a, b, dims):
    return lax.dot_general(a, b, dims, preferred_element_type=F32)


def call(body, outs, *args, flops=0, after=(), far=False, scratch=(), mib=24, far_out=0):
    size = sum(a.size * a.dtype.itemsize for a in args) + sum(o.size * o.dtype.itemsize for o in outs)
    count = len(args)

    def run(*refs):
        body(*refs[:count], *refs[count + len(after) :])

    return pl.pallas_call(
        run,
        out_shape=outs,
        in_specs=[pl.BlockSpec(memory_space=pltpu.HBM if far else pltpu.VMEM)] * len(args)
        + [pl.BlockSpec(memory_space=pl.ANY)] * len(after),
        out_specs=[pl.BlockSpec(memory_space=pltpu.VMEM)] * (len(outs) - far_out) + [pl.BlockSpec(memory_space=pltpu.HBM)] * far_out,
        scratch_shapes=list(scratch),
        cost_estimate=pl.CostEstimate(flops=flops, bytes_accessed=size, transcendentals=0),
        compiler_params=pltpu.CompilerParams(vmem_limit_bytes=int(mib * 1024 * 1024)),
    )(*args, *after)


def arr(shape, dtype=BF):
    return jax.ShapeDtypeStruct(shape, dtype)


def pack_body(picks_in, scores_in, tok_in, grad_in, gate_in, up_in, down_in, xd_ref, sel_ref, w_out, picks_ref, scores_ref, tok_ref, grad_ref, sems):
    pairs = [(picks_in, picks_ref), (scores_in, scores_ref), (tok_in, tok_ref), (grad_in, grad_ref)]
    h = gate_in.shape[0]
    pairs += [(w, w_out.at[i * h : (i + 1) * h]) for i, w in enumerate((gate_in, up_in, down_in))]
    copies = [pltpu.make_async_copy(a, b, sems.at[i]) for i, (a, b) in enumerate(pairs)]
    for c in copies:
        c.start()
    tok_dev = tok_ref.shape[0]
    cap = picks_ref.shape[1]
    base = lax.axis_index("seq") * tok_dev
    before = (
        lax.broadcasted_iota(jnp.int32, (tok_dev, tok_dev), 0) < lax.broadcasted_iota(jnp.int32, (tok_dev, tok_dev), 1)
    ).astype(F32).astype(BF)
    slots = lax.broadcasted_iota(jnp.int32, (MOST, tok_dev), 0).astype(F32)
    copies[0].wait()
    where = picks_ref[...] - base
    hit = (lax.broadcasted_iota(jnp.int32, (tok_dev, cap), 0) == where).astype(F32).astype(BF)
    picked = dot(jnp.ones((8, cap), BF), hit, NT)
    rank = dot(picked.astype(BF), before, NN)[0:1]
    sel = jnp.where((rank == slots) & (picked[0:1] > 0.5), 1.0, 0.0).astype(BF)
    sel_ref[...] = sel
    chosen = dot(sel, hit, NN)
    copies[1].wait()
    score = jnp.sum(chosen * scores_ref[...], axis=1, keepdims=True)
    copies[2].wait()
    xd_ref[0:MOST] = dot(sel, tok_ref[...], NN).astype(BF)
    copies[3].wait()
    xd_ref[MOST:] = (score * dot(sel, grad_ref[...], NN)).astype(BF)
    for c in copies[4:]:
        c.wait()


def partial_body(blocks, rows, *refs):
    w_own, w_oth, keep_ref, send_ref = refs[blocks : blocks + 4]
    h = w_own.shape[0] // 3
    done = 0
    for at, half in rows:
        a = jnp.concatenate([r[half * MOST : (half + 1) * MOST] for r in refs[:blocks]], axis=0)
        part = jnp.concatenate([dot(w[at[0] * h : at[1] * h], a, NT) for w in (w_own, w_oth)], axis=1)
        keep_ref[done : done + part.shape[0]] = part
        send_ref[done : done + part.shape[0]] = part.astype(BF)
        done += part.shape[0]


def terms(keep, recv, dd_ref):
    both = [jnp.concatenate([r[...].astype(F32) for r in refs], axis=0) for refs in (keep, recv)]
    h = both[0].shape[0] // 3
    gate, upper, d_act = (both[0][i * h : (i + 1) * h] + both[1][i * h : (i + 1) * h] for i in range(3))
    sigma = jax.nn.sigmoid(gate)
    gs = gate * sigma
    dd_ref[0:h] = (d_act * upper * sigma * (1.0 + gate * (1.0 - sigma))).astype(BF)
    dd_ref[h : 2 * h] = (d_act * gs).astype(BF)
    dd_ref[2 * h :] = (gs * upper).astype(BF)


def back_rows(dd, w_own, w_oth, dx_refs):
    at = slice(0, 2 * w_own.shape[0] // 3)
    m = dd.shape[1] // 2
    total = dot(dd[at], w_own[at], TN)[0:m] + dot(dd[at], w_oth[at], TN)[m:]
    for s, ref in enumerate(dx_refs):
        ref[...] = total[s * MOST : (s + 1) * MOST].astype(BF)


def first_body(parts, *refs):
    w_own, w_oth, dd_ref, *dx_refs = refs[2 * parts :]
    terms(refs[:parts], refs[parts : 2 * parts], dd_ref)
    back_rows(dd_ref, w_own, w_oth, dx_refs)


def second_body(blocks, parts, *refs):
    keep, recv = refs[:parts], refs[parts : 2 * parts]
    w_own, w_oth, dd_a, *refs = refs[2 * parts :]
    early, refs = refs[: blocks // 2], refs[blocks // 2 :]
    dd_ref, rows_ref, *dx_refs = refs[blocks:]
    m = dd_a.shape[1]
    terms(keep, recv, dd_ref.at[:, m:])
    back_rows(dd_ref.at[:, m:], w_own, w_oth, dx_refs[len(early) :])
    for a, ref in zip(early, dx_refs):
        ref[...] = a[...]
    dd_ref[:, 0:m] = dd_a[...]
    for s, block in enumerate(refs[:blocks]):
        rows_ref[s * MOST : (s + 1) * MOST] = block[0:MOST]
        rows_ref[(blocks + s) * MOST : (blocks + s + 1) * MOST] = block[MOST:]


def weights_body(coeff, rows_own, rows_oth, own, oth, gate_ref, up_ref, down_ref, token_ref):
    h = gate_ref.shape[0]
    m = rows_own.shape[0] // 4
    zero = jnp.zeros((m, rows_own.shape[1]), BF)
    for i, out in enumerate((gate_ref, up_ref, down_ref)):
        at = slice(i * h, (i + 1) * h)
        r = 0 if i < 2 else 2 * m
        mine = jnp.concatenate([rows_own[r : r + m], zero, rows_own[r + m : r + 2 * m], zero], axis=0)
        others = jnp.concatenate([zero, rows_oth[r : r + m], zero, rows_oth[r + m : r + 2 * m]], axis=0)
        one = dot(own[at], mine, NN)
        two = dot(oth[at], others, NN)
        out[...] = ((coeff * one).astype(BF).astype(F32) + (coeff * two).astype(BF).astype(F32)).astype(BF)
    token_ref[...] = jnp.zeros_like(token_ref)


def spread_body(sel_ref, *refs):
    total = refs[0][...].astype(F32)
    for r in refs[1:-1]:
        total += r[...].astype(F32)
    refs[-1][...] = dot(sel_ref[...], total.astype(BF), TN).astype(BF)


def swapped(tokens, grad_out, picks, scores, w_gate, w_up, w_down):
    n = lax.axis_size("seq")
    replicas = lax.axis_size("dp")
    tok_dev, half = tokens.shape[1:]
    cap = picks.shape[1]
    h = w_gate.shape[1]
    m = n // 2 * MOST
    coeff = float(replicas * cap) ** -0.5

    def index(d, k, t):
        return (k * 2 + d) * 2 + t

    def across(x, s):
        pairs = [(index(d, k, t), index(t, k ^ s, d)) for d in range(2) for k in range(n) for t in range(2)]
        return lax.ppermute(x, ("seq", "dp", "tensor"), pairs)

    def swap(x, axis):
        return lax.ppermute(x, axis, [(0, 1), (1, 0)])

    xd, sel, w_own = call(
        pack_body,
        [arr((2 * MOST, half)), arr((MOST, tok_dev)), arr((3 * h, half))],
        *(pltpu.with_memory_space_constraint(a, pltpu.HBM) for a in (picks, scores, tokens[0], grad_out[0], w_gate.T, w_up.T, w_down)),
        far=True, mib=24,
        scratch=[pltpu.VMEM((1, cap), jnp.int32), pltpu.VMEM((1, cap), F32), pltpu.VMEM((tok_dev, half), BF),
                 pltpu.VMEM((tok_dev, half), BF), pltpu.SemaphoreType.DMA((7,))],
    )
    blocks = {s: across(xd, s) for s in (2, 1, 0)}
    blocks[3] = lax.ppermute(blocks[2], "seq", [(k, k ^ 1) for k in range(n)])
    w_oth = swap(w_own, "tensor")
    flops = 2 * m * half * h

    def partial(group, *parts):
        keep, send = [], []
        for rows in parts:
            size = sum(at[1] - at[0] for at, _ in rows) * h
            a, b = call(
                functools.partial(partial_body, len(group), rows), [arr((size, 2 * m), F32), arr((size, 2 * m))],
                *(blocks[s] for s in group), w_own, w_oth, flops=6 * flops, after=keep[-1:],
            )
            keep.append(a)
            send.append(swap(b, "dp"))
        return keep, send

    near, far = (1, 2), (0, 3)
    products, slopes = ((0, 2), 0), ((2, 3), 1)
    dx = [arr((MOST, half))] * (n // 2)
    keep_a, recv_a = partial(near, (products, slopes))
    keep_b, recv_b = partial(far, (products,), (slopes,))
    dd_a, *dx_a = call(
        functools.partial(first_body, len(keep_a)), [arr((3 * h, 2 * m))] + dx,
        *keep_a, *recv_a, w_own, w_oth, flops=8 * flops, after=keep_b[-1:],
    )
    own, rows_own, *dx = call(
        functools.partial(second_body, n, len(keep_b)), [arr((3 * h, 4 * m)), arr((2 * n * MOST, half))] + dx * 2,
        *keep_b, *recv_b, w_own, w_oth, dd_a, *dx_a, *(blocks[s] for s in (*near, *far)), flops=8 * flops,
    )
    back = {s: across(b, s) for s, b in zip((*near, *far), dx)}
    rows_oth, oth = swap(rows_own, "tensor"), swap(own, "tensor")
    grads = call(
        functools.partial(weights_body, coeff), [arr((h, half))] * 3 + [arr((8, 128), F32)],
        rows_own, rows_oth, own, oth, flops=12 * flops,
    )
    (grad_local,) = call(spread_body, [arr((tok_dev, half))], sel, *(back[s] for s in (2, 3, 1, 0)), after=grads[3:])
    return grad_local[None], grads[0].T, grads[1].T, grads[2]


def gathered(tokens, grad_out, picks, scores, w_gate, w_up, w_down):
    tok_dev = tokens.shape[1]
    half = tokens.shape[2]
    seq_count = lax.axis_size("seq")
    ten_count = lax.axis_size("tensor")
    picks_row = picks[0]
    score_row = scores[0]
    cap = picks_row.shape[0]
    each = cap // (seq_count * ten_count)
    my_seq = lax.axis_index("seq")
    my_ten = lax.axis_index("tensor")
    my_replica = lax.axis_index("dp")
    share = w_gate.shape[0]
    full_gate, full_up, full_down = (
        lax.all_gather(w_gate, "dp", axis=0, tiled=True),
        lax.all_gather(w_up, "dp", axis=0, tiled=True),
        lax.all_gather(w_down, "dp", axis=1, tiled=True),
    )
    owner = picks_row // tok_dev
    mine = owner == my_seq
    place = jnp.clip(picks_row - my_seq * tok_dev, 0, tok_dev - 1)
    local_rows = tokens[0]
    local_grads = grad_out[0]
    zero_value = jnp.zeros((), jnp.bfloat16)
    shard_ids = jnp.arange(seq_count, dtype=jnp.int32)
    owner_table = (owner[:, None] == shard_ids[None, :]).astype(jnp.int32)
    earlier = jnp.cumsum(owner_table, axis=0) - owner_table
    slot_of = jnp.sum(earlier * owner_table, axis=1)
    slot_ids = jnp.arange(MOST, dtype=jnp.int32)
    match = (mine[None, :] & (slot_of[None, :] == slot_ids[:, None])).astype(jnp.int32)
    pick_ids = jnp.sum(match * jnp.arange(cap, dtype=jnp.int32)[None, :], axis=1)
    valid = jnp.sum(match, axis=1) > 0
    rows_at = jnp.clip(jnp.take(picks_row, pick_ids) - my_seq * tok_dev, 0, tok_dev - 1)
    pack_rows = jnp.where(valid[:, None], jnp.take(local_rows, rows_at, axis=0), zero_value)
    pack_grads = jnp.where(valid[:, None], jnp.take(local_grads, rows_at, axis=0), zero_value)
    all_rows, all_grads = (
        lax.all_gather(pack_rows, ("seq", "tensor"), axis=0, tiled=True),
        lax.all_gather(pack_grads, ("seq", "tensor"), axis=0, tiled=True),
    )

    def unpack(block):
        parts = [
            jnp.take(block, (owner * ten_count + part) * MOST + slot_of, axis=0)
            for part in range(ten_count)
        ]
        return jnp.concatenate(parts, axis=1)

    x_rows = unpack(all_rows)
    dy_rows = unpack(all_grads)
    dz = (score_row[:, None] * dy_rows.astype(jnp.float32)).astype(jnp.bfloat16)
    gate = jnp.dot(x_rows, full_gate, preferred_element_type=jnp.float32)
    upper = jnp.dot(x_rows, full_up, preferred_element_type=jnp.float32)
    sigma = jax.nn.sigmoid(gate)
    act = (gate * sigma * upper).astype(jnp.bfloat16)
    last_dims = (((1,), (1,)), ((), ()))
    first_dims = (((0,), (0,)), ((), ()))
    d_act = lax.dot_general(dz, full_down, last_dims, preferred_element_type=jnp.float32)
    d_gate = (d_act * upper * sigma * (1.0 + gate * (1.0 - sigma))).astype(jnp.bfloat16)
    d_up = (d_act * gate * sigma).astype(jnp.bfloat16)
    result = lax.dot_general(d_gate, full_gate, last_dims, preferred_element_type=jnp.float32)
    summed = lax.psum_scatter(
        result + lax.dot_general(d_up, full_up, last_dims, preferred_element_type=jnp.float32),
        ("seq", "tensor"),
        scatter_dimension=0,
        tiled=True,
    )
    coeff = float(lax.axis_size("dp") * cap) ** (-0.5)
    term_gate = (
        coeff * lax.dot_general(x_rows, d_gate, first_dims, preferred_element_type=jnp.float32)
    ).astype(jnp.bfloat16)
    term_up = (
        coeff * lax.dot_general(x_rows, d_up, first_dims, preferred_element_type=jnp.float32)
    ).astype(jnp.bfloat16)
    term_down = (
        coeff * lax.dot_general(act, dz, first_dims, preferred_element_type=jnp.float32)
    ).astype(jnp.bfloat16)
    sum_gate, sum_up, sum_down = (
        lax.psum(term_gate, "dp").astype(jnp.float32),
        lax.psum(term_up, "dp").astype(jnp.float32),
        lax.psum(term_down, "dp").astype(jnp.float32),
    )
    own_gate = lax.dynamic_slice_in_dim(sum_gate, my_replica * share, share, 0)
    own_up = lax.dynamic_slice_in_dim(sum_up, my_replica * share, share, 0)
    own_down = lax.dynamic_slice_in_dim(sum_down, my_replica * share, share, 1)
    my_block = my_seq * ten_count + my_ten
    block_owner = lax.dynamic_slice_in_dim(owner, my_block * each, each, 0)
    block_rows = summed.astype(jnp.bfloat16).reshape(each, ten_count, half).transpose(1, 0, 2)
    targets = block_owner[None, :] == jnp.arange(seq_count, dtype=jnp.int32)[:, None]
    outgoing = jnp.where(targets[:, None, :, None], block_rows[None], zero_value)
    incoming = lax.all_to_all(
        outgoing.reshape(seq_count * ten_count * each, half),
        ("seq", "tensor"),
        split_axis=0,
        concat_axis=0,
        tiled=True,
    )
    positions = jnp.arange(tok_dev, dtype=jnp.int32)
    selector = ((place[None, :] == positions[:, None]) & mine[None, :]).astype(jnp.bfloat16)
    grad_local = jnp.dot(selector, incoming, preferred_element_type=jnp.float32).astype(
        jnp.bfloat16
    )
    return (
        grad_local.reshape(1, tok_dev, half),
        own_gate.astype(jnp.bfloat16),
        own_up.astype(jnp.bfloat16),
        own_down.astype(jnp.bfloat16),
    )


def solution(mesh):
    in_specs = (
        P(("groups", "dp"), "seq", "tensor"),
        P(("groups", "dp"), "seq", "tensor"),
        P(("groups", "dp"), None),
        P(("groups", "dp"), None),
        P("dp", ("seq", "tensor")),
        P("dp", ("seq", "tensor")),
        P(("seq", "tensor"), "dp"),
    )
    out_specs = (
        P(("groups", "dp"), "seq", "tensor"),
        P(("groups", "dp"), ("seq", "tensor")),
        P(("groups", "dp"), ("seq", "tensor")),
        P(("groups", "seq", "tensor"), "dp"),
    )
    size = mesh.shape
    pairs = size["dp"] == size["tensor"] == 2 and size["seq"] == 4
    local = swapped if pairs else gathered
    return jax.shard_map(local, mesh=mesh, in_specs=in_specs, out_specs=out_specs, check_vma=False)
```
